128 devices in a mesh: expert: 32 (over y, z, core), tensor: 4 (over x).
Axes of the slice: x: 4, y: 4, z: 4, core: 2. Of those that a mesh axis runs over, the one named last changes fastest.
Arguments:
- tokens: bfloat16 [1024, 7168], P('expert'), may hold values from -6 to 6
- cotangent: bfloat16 [1024, 7168], P('expert'), may hold values from -1.5 to 1.5
- gate_weights: bfloat16 [1024, 8], P('expert'), may hold values from 0.019897461 to 0.5
- route_slots: int32 [1024, 8], P('expert'), may hold values from 0 to 31, all different within a row; in each aligned block of 32 rows (0 to 31, 32 to 63, ...) at most 12 rows name the same one
- replica_owner: int32 [4], replicated, may hold values from 0 to 27, as said below
- w_gate: bfloat16 [32, 7168, 1024], P('expert', None, 'tensor'), as said below
- w_up: bfloat16 [32, 7168, 1024], P('expert', None, 'tensor'), as said below
- w_down: bfloat16 [32, 7168, 1024], P('expert', None, 'tensor'), as said below
Outputs:
- input_grads: bfloat16 [1024, 7168], P('expert', 'tensor')
- gate_grads: bfloat16 [1024, 8], P('expert')
- expert_grads: bfloat16 [28, 7168, 3, 1024], P(None, 'expert', None, 'tensor')
The draws below stay inside these ranges and needn't reach their ends.
Inputs may be any that keep to these rules, and one draw needn't show every extreme that they name: `route_slots`: in each block of 32 tokens no slot is named by more than 12 entries, a bound that some block reaches; a token names 8 different slots. `replica_owner`: numbers of experts; one expert may own several replicas, and a replica slot's weights equal its expert's. `w_gate`: slot 28 + r holds the same matrix as slot replica_owner[r]. `w_up`: slot 28 + r holds the same matrix as slot replica_owner[r]. `w_down`: slot 28 + r holds the same matrix as slot replica_owner[r].
All inputs are finite; a program needn't handle non-finite values.
Results may differ from the reference program's by a relative error of at most 0.012.
Values may be sent and summed in bfloat16 or wider, within the bound.
A program may use at most 128 MiB of HBM per device.

```python
import math
import jax
import jax.numpy as jnp
import numpy as np
from jax import lax

D = 7168
TOP = 8
FF = 1024
TOK_DEV = 32
TOKENS = 1024
ROWS = 384
CAP = 12
REPLICAS = 4
LOGICAL = 28
N_EXPERT = 32
N_TENSOR = 4


def replica_table(key):
    hot_expert = jax.random.randint(jax.random.fold_in(key, 5), (1,), 0, LOGICAL, dtype=jnp.int32)
    spread = jax.random.randint(jax.random.fold_in(key, 6), (REPLICAS,), 0, LOGICAL, dtype=jnp.int32)
    coins = jax.random.randint(jax.random.fold_in(key, 7), (REPLICAS,), 0, 2, dtype=jnp.int32)
    owners = jnp.where(coins == 1, hot_expert, spread).astype(jnp.int32)
    last_mark = jnp.arange(REPLICAS, dtype=jnp.int32) == REPLICAS - 1
    owners = jnp.where(last_mark, jnp.int32(LOGICAL - 1), owners).astype(jnp.int32)
    return jnp.concatenate([jnp.arange(LOGICAL, dtype=jnp.int32), owners])


def tied_weights(key, salt, fan_in):
    slot_table = replica_table(key)
    shape = (LOGICAL, D, FF)
    base = jax.random.normal(jax.random.fold_in(key, salt), shape, jnp.float32)
    return (base[slot_table] * fan_in ** (-0.5)).astype(jnp.bfloat16)


def draw_replica_owner(key, part):
    return replica_table(key)[LOGICAL:]


def draw_w_gate(key, part):
    return tied_weights(key, 11, D)


def draw_w_up(key, part):
    return tied_weights(key, 12, D)


def draw_w_down(key, part):
    return tied_weights(key, 13, FF)


def block_levels(key, dims, shards, least, largest):
    gain = 1.0
    for dim, blocks in shards:
        heights = jax.random.uniform(jax.random.fold_in(jax.random.fold_in(key, 6), dim), (blocks,), jnp.float32, least / len(shards), largest / len(shards))
        gain = gain * jnp.repeat(jnp.exp(heights), dims[dim] // blocks).reshape((-1,) + (1,) * (len(dims) - 1 - dim))
    return gain


def shared_out(rng, own, number, rows, amount, top, reach, lean):
    order = jax.random.permutation(rng, amount)
    packed, common = load_shares(amount, rows * top, reach, lean, True), load_shares(amount, rows * top, reach, lean, False)
    places = jnp.arange(amount)

    def named(lengths, turn):
        used = int((lengths > 0).sum())
        fixed = max(1, used // 4)
        moved = fixed + (places - fixed + turn * (used - fixed)) % max(1, amount - fixed)
        return jnp.zeros((amount,), jnp.int32).at[order[jnp.where(places < fixed, places, moved)]].set(jnp.asarray(lengths, jnp.int32))

    lengths = jnp.where(number % 4 == 0, named(packed, number // 4), named(common, number - number // 4 - 1))
    mixed = jax.random.permutation(jax.random.fold_in(own, 3), amount)
    donor, receiver = mixed[0:amount // 2 * 2:2], mixed[1:amount // 2 * 2:2]
    room = jnp.minimum(lengths[donor] - 1, reach - lengths[receiver]) // 2
    room = jnp.where((donor == order[0]) | (receiver == order[0]) | (lengths[receiver] == 0), 0, jnp.maximum(room, 0))
    moved = jax.random.randint(jax.random.fold_in(own, 4), (amount // 2,), 0, 1 << 20) % (room + 1)
    lengths = lengths.at[donor].add(-moved).at[receiver].add(moved)
    labels = jnp.searchsorted(jnp.cumsum(lengths), jnp.arange(rows * top), side="right").astype(jnp.int32)
    listing = labels.reshape(top, rows).T
    listing = listing[jax.random.permutation(jax.random.fold_in(own, 1), rows)]
    turn = jax.random.randint(jax.random.fold_in(own, 2), (rows, 1), 0, top)
    return jnp.take_along_axis(listing, (jnp.arange(top)[None, :] + turn) % top, axis=1)


def load_shares(number_of, total, reach, lean, full):
    loads = [(1 << 20) // math.isqrt(standing ** lean) + 1 for standing in range(1, number_of + 1)]
    largest = reach if full else min(reach, max(-(-total // number_of), total * loads[0] // sum(loads)))
    least = 1 if total - largest >= number_of - 1 else 0
    counts, rest = [largest] + [least] * (number_of - 1), total - largest - least * (number_of - 1)
    while rest > 0:
        candidates = [i for i in range(1, number_of) if counts[i] < largest] or [i for i in range(1, number_of) if counts[i] < reach]
        whole, budget = sum([loads[i] for i in candidates]), rest
        for i in candidates:
            more = min(reach - counts[i], max(1, budget * loads[i] // whole), rest)
            counts[i] = counts[i] + more
            rest = rest - more
    return np.array(counts)


def gaussian(rng, extent, deviation, reach, cuts=(), kind=jnp.bfloat16):
    drawn = jax.random.normal(rng, extent, jnp.float32) * deviation
    if len(cuts) > 0:
        drawn = block_levels(rng, extent, cuts, -0.22, 0.18) * drawn
    return jnp.clip(drawn, min=-reach, max=reach).astype(kind)


def setup_inputs(seed: int = 0) -> dict:
    arg_keys = jax.random.split(jax.random.key(seed), 9)
    tokens = gaussian(arg_keys[0], (TOKENS, D), 1.0, 6.0, ((0, 32),))
    cotangent = gaussian(arg_keys[1], (TOKENS, D), 0.25, 1.5, ((0, 32),))
    gate_weights = jnp.clip(jnp.exp(math.log(0.5) - 3.224016 * jax.random.uniform(arg_keys[2], (TOKENS, TOP), jnp.float32) ** block_levels(arg_keys[2], (TOKENS, TOP), ((0, 32),), -0.2, 0.2)), 0.019897461, 0.5).astype(jnp.bfloat16)
    route_slots_keys = jax.random.split(jax.random.fold_in(arg_keys[3], 1), TOKENS // TOK_DEV)
    route_slots_turns = jax.random.permutation(jax.random.fold_in(arg_keys[3], 3), TOKENS // TOK_DEV)
    route_slots = jax.vmap(lambda own, number: shared_out(jax.random.fold_in(arg_keys[3], 2), own, number, TOK_DEV, N_EXPERT, TOP, CAP, 2))(route_slots_keys, route_slots_turns).reshape((TOKENS, TOP))
    replica_owner = draw_replica_owner(jax.random.fold_in(arg_keys[8], 71), 0)
    w_gate = draw_w_gate(jax.random.fold_in(arg_keys[8], 71), 0)
    w_up = draw_w_up(jax.random.fold_in(arg_keys[8], 71), 0)
    w_down = draw_w_down(jax.random.fold_in(arg_keys[8], 71), 0)
    return {"tokens": tokens, "cotangent": cotangent, "gate_weights": gate_weights, "route_slots": route_slots, "replica_owner": replica_owner, "w_gate": w_gate, "w_up": w_up, "w_down": w_down}


def dispatch_targets(route_block, slot_total, capacity):
    flat_ids = route_block.reshape(-1)
    one_hot = (flat_ids[:, None] == jnp.arange(slot_total, dtype=jnp.int32)[None, :]).astype(jnp.int32)
    earlier = jnp.cumsum(one_hot, axis=0) - 1
    position = jnp.sum(one_hot * earlier, axis=1)
    return (flat_ids * capacity + position).reshape(route_block.shape).astype(jnp.int32)


def reference(tokens, cotangent, gate_weights, route_slots, replica_owner, w_gate, w_up, w_down):
    token_blocks = tokens.reshape(N_EXPERT, TOK_DEV, D).astype(jnp.float32)
    cot_blocks = cotangent.reshape(N_EXPERT, TOK_DEV, D).astype(jnp.float32)
    route_blocks = route_slots.reshape(N_EXPERT, TOK_DEV, TOP)
    gate_blocks = gate_weights.reshape(N_EXPERT, TOK_DEV, TOP).astype(jnp.float32)
    targets = jax.vmap(lambda block: dispatch_targets(block, N_EXPERT, CAP))(route_blocks)
    matches = targets[:, None, :, :] == jnp.arange(ROWS, dtype=jnp.int32)[None, :, None, None]
    select = jnp.any(matches, axis=3)
    select_f = select.astype(jnp.float32)
    gate_send = jnp.sum(jnp.where(matches, gate_blocks[:, None, :, :], 0.0), axis=(2, 3)).astype(jnp.bfloat16)
    quarter = FF // N_TENSOR

    def expert_step(slot):
        picked = lax.dynamic_slice_in_dim(select_f, slot * CAP, CAP, 1)
        x_rows = jnp.einsum("bct,btd->bcd", picked, token_blocks).reshape(ROWS, D).astype(jnp.bfloat16)
        dy_rows = jnp.einsum("bct,btd->bcd", picked, cot_blocks).reshape(ROWS, D).astype(jnp.bfloat16)
        g_rows = lax.dynamic_slice_in_dim(gate_send, slot * CAP, CAP, 1).reshape(ROWS)
        gate_mat = w_gate[slot]
        up_mat = w_up[slot]
        down_mat = w_down[slot]
        gate_proj = jnp.dot(x_rows, gate_mat, preferred_element_type=jnp.float32)
        up_proj = jnp.dot(x_rows, up_mat, preferred_element_type=jnp.float32)
        sigmoid_gate = jax.nn.sigmoid(gate_proj)
        activated = gate_proj * sigmoid_gate
        hidden = (activated * up_proj).astype(jnp.bfloat16)
        expert_out = jnp.dot(hidden, down_mat.T, preferred_element_type=jnp.float32)
        row_score = jnp.sum(dy_rows.astype(jnp.float32) * expert_out, axis=1).astype(jnp.bfloat16)
        scaled = (g_rows.astype(jnp.float32)[:, None] * dy_rows.astype(jnp.float32)).astype(jnp.bfloat16)
        hidden_grad = jnp.dot(scaled, down_mat, preferred_element_type=jnp.float32)
        up_grad = (hidden_grad * activated).astype(jnp.bfloat16)
        pre_grad = (hidden_grad * up_proj * sigmoid_gate * (1.0 + gate_proj * (1.0 - sigmoid_gate))).astype(jnp.bfloat16)
        grad_gate = jnp.dot(x_rows.T, pre_grad, preferred_element_type=jnp.float32)
        grad_up = jnp.dot(x_rows.T, up_grad, preferred_element_type=jnp.float32)
        grad_down = jnp.dot(scaled.T, hidden, preferred_element_type=jnp.float32)
        slot_grads = jnp.stack([grad_gate, grad_up, grad_down], axis=1).astype(jnp.bfloat16)
        input_sum = jnp.zeros((ROWS, D), jnp.float32)
        for block in range(N_TENSOR):
            lower = block * quarter
            upper = lower + quarter
            term = jnp.dot(pre_grad[:, lower:upper], gate_mat[:, lower:upper].T, preferred_element_type=jnp.float32)
            term = term + jnp.dot(up_grad[:, lower:upper], up_mat[:, lower:upper].T, preferred_element_type=jnp.float32)
            input_sum = input_sum + lax.optimization_barrier(term.astype(jnp.bfloat16)).astype(jnp.float32)
        return row_score, input_sum.astype(jnp.bfloat16), slot_grads

    replica_out = lax.map(expert_step, LOGICAL + jnp.arange(REPLICAS, dtype=jnp.int32))

    def primary_step(expert):
        row_score, row_input, slot_grads = expert_step(expert)
        owned = (replica_owner == expert)[:, None, None, None]
        total = slot_grads.astype(jnp.float32) + jnp.sum(jnp.where(owned, replica_out[2].astype(jnp.float32), 0.0), axis=0)
        return row_score, row_input, total.astype(jnp.bfloat16)

    primary_out = lax.map(primary_step, jnp.arange(LOGICAL, dtype=jnp.int32))
    score_all = jnp.concatenate([primary_out[0], replica_out[0]], axis=0)
    input_all = jnp.concatenate([primary_out[1], replica_out[1]], axis=0)

    def return_block(source):
        back_rows = lax.dynamic_slice_in_dim(input_all, source * CAP, CAP, 1).reshape(ROWS, D)
        back_score = lax.dynamic_slice_in_dim(score_all, source * CAP, CAP, 1).reshape(ROWS)
        select_block = select[source].astype(jnp.bfloat16)
        grad_rows = lax.dot_general(select_block, back_rows, ((((0,), (0,))), ((), ())), preferred_element_type=jnp.float32)
        grad_gate = back_score[targets[source]]
        return grad_rows.astype(jnp.bfloat16), grad_gate

    grad_rows, grad_gate = lax.map(return_block, jnp.arange(N_EXPERT, dtype=jnp.int32))
    return grad_rows.reshape(TOKENS, D), grad_gate.reshape(TOKENS, TOP), primary_out[2]
```

```python
import jax
import jax.numpy as jnp
from jax import lax
from jax.sharding import PartitionSpec as P

PAD = 128


def places_of(route, slots, blocks):
    tokens = route.shape[0]
    hit = jnp.sum(
        (route[:, :, None] == jnp.arange(slots, dtype=route.dtype)[None, None, :]).astype(
            jnp.bfloat16
        ),
        axis=1,
    )
    per = tokens // blocks
    earlier = (
        lax.broadcasted_iota(jnp.int32, (per, per), 1)
        < lax.broadcasted_iota(jnp.int32, (per, per), 0)
    ).astype(jnp.bfloat16)
    place = jnp.einsum(
        "ij,bjs->bis",
        earlier,
        hit.reshape(blocks, per, slots),
        preferred_element_type=jnp.float32,
    ).reshape(tokens, slots)
    return hit, place


def per_device(tokens, cotangent, gate_weights, route_slots, replica_owner, w_gate, w_up, w_down):
    slots = lax.axis_size("expert")
    tensor_total = lax.axis_size("tensor")
    me = lax.axis_index("expert")
    per, width = tokens.shape
    top = route_slots.shape[1]
    cap = per * top * 3 // 2 // slots
    rows = cap * slots
    part = width // tensor_total
    group = 8
    groups = slots // group
    extra = jnp.concatenate(
        [
            route_slots.astype(jnp.bfloat16),
            gate_weights,
            jnp.zeros((per, PAD - 2 * top), jnp.bfloat16),
        ],
        axis=1,
    )
    x_all = lax.all_gather(
        jnp.concatenate([tokens, extra], axis=1), "expert", axis=0, tiled=True
    )
    dy_all = lax.all_gather(cotangent, "expert", axis=0, tiled=True)
    total = x_all.shape[0]
    route = x_all[:, width : width + top].astype(jnp.int32)
    gates = x_all[:, width + top : width + 2 * top]
    hit, place = places_of(route, slots, slots)
    block_in_group = (jnp.arange(total, dtype=jnp.int32) // per) % group
    row_at = jnp.where(
        hit > 0, block_in_group[:, None] * cap + place.astype(jnp.int32), -1
    ).reshape(groups, group * per, slots)
    gate_at = jnp.sum(
        jnp.where(
            route[:, :, None] == jnp.arange(slots, dtype=jnp.int32)[None, None, :],
            gates.astype(jnp.float32)[:, :, None],
            0.0,
        ),
        axis=1,
    ).reshape(groups, group * per, slots)
    lane = jnp.arange(group * cap, dtype=jnp.int32)
    mine = lax.dynamic_slice_in_dim(row_at, me, 1, 2)[:, :, 0]
    my_gate = lax.dynamic_slice_in_dim(gate_at, me, 1, 2)[:, :, 0]
    pick = mine[:, None, :] == lane[None, :, None]
    select = pick.astype(jnp.bfloat16)
    g_rows = jnp.sum(jnp.where(pick, my_gate[:, None, :], 0.0), axis=2).reshape(rows)

    def rows_of(whole):
        return jnp.einsum(
            "grt,gtd->grd",
            select,
            whole.reshape(groups, group * per, width),
            preferred_element_type=jnp.float32,
        ).astype(jnp.bfloat16).reshape(rows, width)

    x_rows = rows_of(x_all[:, :width])
    dy_rows = rows_of(dy_all)
    gate_mat, up_mat, down_mat = w_gate[0], w_up[0], w_down[0]
    gate_proj = jnp.dot(x_rows, gate_mat, preferred_element_type=jnp.float32)
    up_proj = jnp.dot(x_rows, up_mat, preferred_element_type=jnp.float32)
    down_proj = jnp.dot(dy_rows, down_mat, preferred_element_type=jnp.float32)
    sigmoid_gate = jax.nn.sigmoid(gate_proj)
    activated = gate_proj * sigmoid_gate
    hidden_f = activated * up_proj
    hidden = hidden_f.astype(jnp.bfloat16)
    score = jnp.sum(hidden.astype(jnp.float32) * down_proj, axis=1)
    hidden_grad = g_rows[:, None] * down_proj
    up_grad = (hidden_grad * activated).astype(jnp.bfloat16)
    pre_grad = (
        hidden_grad * up_proj * sigmoid_gate * (1.0 + gate_proj * (1.0 - sigmoid_gate))
    ).astype(jnp.bfloat16)
    acts = lax.all_gather(
        jnp.concatenate([pre_grad, up_grad, hidden], axis=1), "expert", axis=0, tiled=False
    )
    contract_hidden = (((1,), (1,)), ((), ()))
    input_part = lax.dot_general(
        pre_grad, gate_mat, contract_hidden, preferred_element_type=jnp.float32
    ) + lax.dot_general(up_grad, up_mat, contract_hidden, preferred_element_type=jnp.float32)
    row_input = lax.psum_scatter(
        input_part.astype(jnp.bfloat16), "tensor", scatter_dimension=1, tiled=True
    )
    row_score = lax.psum(score, "tensor").astype(jnp.bfloat16)
    back = lax.all_to_all(
        jnp.concatenate(
            [
                row_input.reshape(slots, cap, part),
                jnp.broadcast_to(row_score.reshape(slots, cap, 1), (slots, cap, PAD)),
            ],
            axis=2,
        ),
        "expert",
        0,
        0,
        tiled=True,
    ).reshape(rows, part + PAD)
    own_route = route_slots
    own_hit, own_place = places_of(own_route, slots, 1)
    own_row = jnp.where(
        own_hit > 0,
        jnp.arange(slots, dtype=jnp.int32)[None, :] * cap + own_place.astype(jnp.int32),
        -1,
    )
    entry_row = jnp.sum(
        jnp.where(
            own_route[:, :, None] == jnp.arange(slots, dtype=jnp.int32)[None, None, :],
            own_row[:, None, :],
            0,
        ),
        axis=2,
    )
    own_matches = entry_row[:, :, None] == jnp.arange(rows, dtype=jnp.int32)[None, None, :]
    own_select = jnp.any(own_matches, axis=1).astype(jnp.bfloat16)
    input_grads = jnp.dot(
        own_select, back[:, :part], preferred_element_type=jnp.float32
    ).astype(jnp.bfloat16)
    gate_grads = jnp.sum(
        jnp.where(own_matches, back[:, part].astype(jnp.float32)[None, None, :], 0.0), axis=2
    ).astype(jnp.bfloat16)
    own_width = width // slots
    x_cut = lax.dynamic_slice_in_dim(x_all, me * own_width, own_width, 1)
    dy_cut = lax.dynamic_slice_in_dim(dy_all, me * own_width, own_width, 1)
    picks = (
        jnp.transpose(row_at, (0, 2, 1))[:, :, None, :] == lane[None, None, :, None]
    )
    x_slot = jnp.einsum(
        "gsrt,gtd->sgrd",
        picks.astype(jnp.bfloat16),
        x_cut.reshape(groups, group * per, own_width),
        preferred_element_type=jnp.float32,
    ).astype(jnp.bfloat16).reshape(slots, rows, own_width)
    gate_picks = jnp.where(picks, jnp.transpose(gate_at, (0, 2, 1))[:, :, None, :], 0.0)
    dy_slot = jnp.einsum(
        "gsrt,gtd->sgrd",
        gate_picks.astype(jnp.bfloat16),
        dy_cut.reshape(groups, group * per, own_width),
        preferred_element_type=jnp.float32,
    ).astype(jnp.bfloat16).reshape(slots, rows, own_width)
    ff = gate_mat.shape[1]
    in_grads = jnp.einsum(
        "srd,srf->sdf", x_slot, acts[:, :, : 2 * ff], preferred_element_type=jnp.float32
    )
    down_grads = jnp.einsum(
        "srd,srf->sdf", dy_slot, acts[:, :, 2 * ff :], preferred_element_type=jnp.float32
    )
    slot_grads = jnp.stack(
        [in_grads[:, :, :ff], in_grads[:, :, ff:], down_grads], axis=1
    ).astype(jnp.bfloat16)
    experts = slots - replica_owner.shape[0]
    table = jnp.concatenate([jnp.arange(experts, dtype=jnp.int32), replica_owner])
    combine = (table[None, :] == jnp.arange(experts, dtype=jnp.int32)[:, None]).astype(
        jnp.bfloat16
    )
    expert_grads = jnp.einsum(
        "es,skaf->ekaf", combine, slot_grads, preferred_element_type=jnp.float32
    ).astype(jnp.bfloat16)
    return input_grads, gate_grads, jnp.transpose(expert_grads, (0, 2, 1, 3))


def solution(mesh):
    in_specs = (
        P("expert", None),
        P("expert", None),
        P("expert", None),
        P("expert", None),
        P(),
        P("expert", None, "tensor"),
        P("expert", None, "tensor"),
        P("expert", None, "tensor"),
    )
    out_specs = (P("expert", "tensor"), P("expert", None), P(None, "expert", None, "tensor"))
    return jax.shard_map(
        per_device, mesh=mesh, in_specs=in_specs, out_specs=out_specs, check_vma=False
    )
```

```python
import functools

import jax
import jax.numpy as jnp
from jax import lax
from jax.experimental import pallas as pl
from jax.experimental.pallas import tpu as pltpu
from jax.sharding import PartitionSpec as P

MESH = pl.DeviceIdType.MESH
BF = jnp.bfloat16
F32 = jnp.float32
LANE = 128
RING = 4
CORES = 2
MIB = 1 << 20
NT = (((1,), (1,)), ((), ()))
TN = (((0,), (0,)), ((), ()))


def dot(a, b, dims=None):
    if dims is None:
        return jnp.dot(a, b, preferred_element_type=F32)
    return lax.dot_general(a, b, dims, preferred_element_type=F32)


def up1(v):
    return lax.rem(v + 1, RING)


def down1(v):
    return lax.rem(v + RING - 1, RING)


def position():
    e = lax.axis_index("expert")
    t = lax.axis_index("tensor")
    return lax.div(e, CORES * RING), lax.rem(lax.div(e, CORES), RING), lax.rem(e, CORES), t


class Links:
    def __init__(self, send, recv):
        self.send, self.recv, self.count, self.started = send, recv, 0, []
        self.y, self.z, self.c, self.t = position()

    def to(self, y=None, z=None, c=None, t=None):
        y = self.y if y is None else y
        z = self.z if z is None else z
        c = self.c if c is None else c
        t = self.t if t is None else t
        return ((y * RING + z) * CORES + c, t)

    def start(self, src, dst, device):
        copy = pltpu.make_async_remote_copy(
            src_ref=src,
            dst_ref=dst,
            send_sem=self.send.at[self.count],
            recv_sem=self.recv.at[self.count],
            device_id=device,
            device_id_type=MESH,
        )
        self.count += 1
        copy.start()
        self.started.append(copy)
        return copy

    def greet(self, devices):
        barrier = pltpu.get_barrier_semaphore()
        for device in devices:
            pl.semaphore_signal(barrier, inc=1, device_id=device, device_id_type=MESH)
        pl.semaphore_wait(barrier, len(devices))

    def plane(self):
        return [
            self.to(y=up1(self.y)),
            self.to(y=down1(self.y)),
            self.to(z=up1(self.z)),
            self.to(z=down1(self.z)),
            self.to(c=1 - self.c),
        ]

    def drain(self):
        for copy in self.started:
            copy.wait_send()


class Gather:
    def __init__(self, links, at, y_first):
        self.l, self.at, self.y_first = links, at, y_first
        self.first = links.y if y_first else links.z
        self.second = links.z if y_first else links.y

    def place(self, first, second, part=None):
        return self.at(first, second, part) if self.y_first else self.at(second, first, part)

    def along_first(self, v):
        return self.l.to(y=v) if self.y_first else self.l.to(z=v)

    def along_second(self, v):
        return self.l.to(z=v) if self.y_first else self.l.to(y=v)

    def copy(self, ref, device):
        return self.l.start(ref, ref, device)

    def hand_over(self, second):
        ref = self.place(slice(None), second)
        return self.copy(ref, self.l.to(c=1 - self.l.c))

    def one(self):
        own = self.place(self.first, self.second)
        self.m1 = self.copy(own, self.along_first(up1(self.first)))
        self.m2 = self.copy(own, self.along_first(down1(self.first)))

    def two(self):
        self.m1.wait_recv()
        self.m3 = self.copy(
            self.place(down1(self.first), self.second, 0), self.along_first(up1(self.first))
        )
        self.m2.wait_recv()
        self.m4 = self.copy(
            self.place(up1(self.first), self.second, 1), self.along_first(down1(self.first))
        )

    def three(self):
        self.m3.wait_recv()
        self.m4.wait_recv()
        line = self.place(slice(None), self.second)
        self.m5 = self.copy(line, self.along_second(up1(self.second)))
        self.m6 = self.copy(line, self.along_second(down1(self.second)))
        self.s = [self.hand_over(self.second)]

    def four(self):
        low, high = down1(self.second), up1(self.second)
        self.m5.wait_recv()
        self.m7 = self.copy(self.place(slice(None), low, 0), self.along_second(high))
        self.s.append(self.hand_over(low))
        self.m6.wait_recv()
        self.m8 = self.copy(self.place(slice(None), high, 1), self.along_second(low))
        self.s.append(self.hand_over(high))

    def five(self):
        self.m7.wait_recv()
        self.m8.wait_recv()
        self.s.append(self.hand_over(up1(up1(self.second))))

    def six(self):
        for copy in self.s:
            copy.wait_recv()


GATHER_COPIES = 12


def entries(meta, slot, per, cap, top):
    count = meta.shape[0]
    pick = (
        lax.broadcasted_iota(jnp.int32, (2 * top, LANE), 0)
        == lax.broadcasted_iota(jnp.int32, (2 * top, LANE), 1)
    ).astype(F32).astype(BF)
    turned = dot(pick, meta, NT)
    slot = slot.astype(F32)
    hit = jnp.zeros((slot.shape[0], count), F32)
    gate = jnp.zeros((slot.shape[0], count), F32)
    for k in range(top):
        same = turned[k : k + 1] == slot
        hit = hit + jnp.where(same, 1.0, 0.0)
        gate = gate + jnp.where(same, turned[top + k : top + k + 1], 0.0)
    earlier = lax.broadcasted_iota(jnp.int32, (count, count), 0)
    token = lax.broadcasted_iota(jnp.int32, (count, count), 1)
    before = jnp.where(
        (earlier < token) & (lax.div(earlier, per) == lax.div(token, per)), 1.0, 0.0
    ).astype(BF)
    place = dot(hit.astype(BF), before)
    block = lax.div(lax.broadcasted_iota(jnp.int32, hit.shape, 1), per).astype(F32)
    row = jnp.where(hit > 0.5, block * cap + place, -1.0)
    return row, gate, turned


def picks(row, group_rows):
    lines = lax.broadcasted_iota(jnp.int32, (group_rows, row.shape[1]), 0).astype(F32)
    return jnp.where(row == lines, 1.0, 0.0)


def dispatch_kernel(
    dims,
    tokens, cotangent, meta, w_gate, w_up, w_down,
    acts, score, cuts, meta_all,
    buf, wg, wu, wd, rows_buf, gate_acc, up_acc, down_acc, select, gate_rows,
    send, recv, local,
):
    per, width, cap, top, ff = dims
    slots = RING * RING * CORES
    group_rows = cap * slots // RING
    line = per * slots // RING
    links = Links(send, recv)
    y, z, c = links.y, links.z, links.c
    me = lax.axis_index("expert")
    x0, dy0 = LANE, LANE + width
    end = LANE + 2 * width
    loads = [
        pltpu.make_async_copy(meta, buf.at[y, z, c, :, pl.ds(0, LANE)], local.at[0]),
        pltpu.make_async_copy(tokens, buf.at[y, z, c, :, pl.ds(x0, width)], local.at[1]),
        pltpu.make_async_copy(cotangent, buf.at[y, z, c, :, pl.ds(dy0, width)], local.at[2]),
    ]
    weights = [
        pltpu.make_async_copy(w_gate, wg, local.at[3]),
        pltpu.make_async_copy(w_up, wu, local.at[4]),
        pltpu.make_async_copy(w_down, wd, local.at[5]),
    ]
    for copy in loads + weights:
        copy.start()
    for copy in loads:
        copy.wait()
    links.greet(links.plane())

    def piece(start, stop, y_first):
        middle = start + (stop - start) // (2 * LANE) * LANE
        spans = {None: (start, stop), 0: (start, middle), 1: (middle, stop)}

        def at(yy, zz, part):
            low, high = spans[part]
            return buf.at[yy, zz, c, :, pl.ds(low, high - low)]

        return Gather(links, at, y_first)

    half = width // 2
    p0 = piece(0, x0 + half, True)
    p1 = piece(x0 + half, dy0, False)
    p2 = piece(dy0, dy0 + half, True)
    p3 = piece(dy0 + half, end, False)
    p0.one()
    p1.one()
    p0.two()
    p1.two()
    p2.one()
    p3.one()
    p0.three()
    p1.three()
    p2.two()
    p3.two()
    p0.four()
    p1.four()
    p2.three()
    p3.three()
    p0.five()
    p1.five()
    p0.six()
    p1.six()

    for copy in weights:
        copy.wait()
    my_slot = jnp.full((8, 1), me, jnp.int32)
    for g in range(RING):
        part = buf[g, :, :, :, pl.ds(0, LANE)].reshape(line, LANE)
        meta_all[pl.ds(g * line, line), :] = part
        row, gate, _ = entries(part, my_slot, per, cap, top)
        chosen = picks(row[0:1], group_rows)
        select[g] = chosen.astype(BF)
        gate_rows[pl.ds(g * group_rows, group_rows), :] = jnp.broadcast_to(
            jnp.sum(chosen * gate[0:1], axis=1, keepdims=True), (group_rows, LANE)
        )

    chunk = 512

    def fill_rows(start):
        for g in range(RING):
            part = buf[g, :, :, :, pl.ds(start, chunk)].reshape(line, chunk)
            rows_buf[pl.ds(g * group_rows, group_rows), :] = dot(select[g], part).astype(BF)

    gate_acc[...] = jnp.zeros_like(gate_acc)
    up_acc[...] = jnp.zeros_like(up_acc)
    down_acc[...] = jnp.zeros_like(down_acc)

    def x_step(i, carry):
        off = pl.multiple_of(i * chunk, chunk)
        fill_rows(pl.multiple_of(x0 + i * chunk, LANE))
        gate_acc[...] += dot(rows_buf[...], wg[pl.ds(off, chunk), :])
        up_acc[...] += dot(rows_buf[...], wu[pl.ds(off, chunk), :])
        return carry

    def dy_step(i, carry):
        off = pl.multiple_of(i * chunk, chunk)
        fill_rows(pl.multiple_of(dy0 + i * chunk, LANE))
        down_acc[...] += dot(rows_buf[...], wd[pl.ds(off, chunk), :])
        return carry

    steps = width // chunk
    lax.fori_loop(0, steps // 2, x_step, 0)
    p2.four()
    p3.four()
    lax.fori_loop(steps // 2, steps, x_step, 0)
    p2.five()
    p3.five()
    p2.six()
    p3.six()
    lax.fori_loop(0, steps, dy_step, 0)

    own = width // slots
    window = 3 * LANE
    low = jnp.minimum(lax.div(me * own, LANE) * LANE, width - window)
    shift = me * own - low
    move = jnp.where(
        lax.broadcasted_iota(jnp.int32, (window, 2 * LANE), 0)
        == lax.broadcasted_iota(jnp.int32, (window, 2 * LANE), 1) + shift,
        1.0,
        0.0,
    ).astype(BF)
    for k, start in enumerate((x0, dy0)):
        for g in range(RING):
            part = buf[g, :, :, :, pl.ds(pl.multiple_of(start + low, LANE), window)]
            cuts[k, pl.ds(g * line, line), :] = dot(part.reshape(line, window), move).astype(BF)

    def finish(i, carry):
        r = pl.ds(pl.multiple_of(i * 32, 32), 32)
        gate_proj, up_proj, down_proj = gate_acc[r, :], up_acc[r, :], down_acc[r, :]
        sig = jax.nn.sigmoid(gate_proj)
        activated = gate_proj * sig
        hidden = (activated * up_proj).astype(BF)
        hidden_grad = gate_rows[r, 0:1] * down_proj
        acts[r, pl.ds(0, ff)] = (
            hidden_grad * up_proj * sig * (1.0 + gate_proj * (1.0 - sig))
        ).astype(BF)
        acts[r, pl.ds(ff, ff)] = (hidden_grad * activated).astype(BF)
        acts[r, pl.ds(2 * ff, ff)] = hidden
        total = jnp.sum(hidden.astype(F32) * down_proj, axis=1, keepdims=True)
        high = total.astype(BF)
        low_part = (total - high.astype(F32)).astype(BF)
        lanes = lax.broadcasted_iota(jnp.int32, (32, LANE), 1)
        score[r, :] = jnp.where(
            lanes < LANE // 2, high.astype(F32), low_part.astype(F32)
        ).astype(BF)
        return carry

    lax.fori_loop(0, cap * slots // 32, finish, 0)
    links.drain()


def return_kernel(
    dims,
    acts, score, w_gate, w_up,
    acts_all, back,
    wg, wu, a, far, up_buf, down_buf, far_in, sum_in, own_buf, score_in,
    send, recv, local,
):
    per, width, cap, top, ff = dims
    slots = RING * RING * CORES
    rows = cap * slots
    part = width // RING
    half = part // 2
    links = Links(send, recv)
    y, z, c, t = links.y, links.z, links.c, links.t
    own = pltpu.make_async_copy(acts, acts_all.at[y, z, c], local.at[0])
    held = pltpu.make_async_copy(acts, a, local.at[1])
    weights = [
        pltpu.make_async_copy(w_gate, wg, local.at[2]),
        pltpu.make_async_copy(w_up, wu, local.at[3]),
    ]
    for copy in [own, held] + weights:
        copy.start()
    own.wait()
    right, left, across = links.to(t=up1(t)), links.to(t=down1(t)), links.to(t=up1(up1(t)))
    links.greet(links.plane() + [right, left, across])

    def piece(start, stop, y_first):
        middle = (start + stop) // 2
        spans = {None: (start, stop), 0: (start, middle), 1: (middle, stop)}

        def at(yy, zz, which):
            low, high = spans[which]
            return acts_all.at[yy, zz, c, pl.ds(low, high - low), :]

        return Gather(links, at, y_first)

    g0 = piece(0, rows // 2, True)
    g1 = piece(rows // 2, rows, False)
    g0.one()
    g1.one()
    held.wait()
    for copy in weights:
        copy.wait()

    def term(quarter, column):
        r = pl.ds(pl.multiple_of(quarter * part + column, LANE), LANE)
        return dot(a[:, 0:ff], wg[r, :], NT) + dot(a[:, ff : 2 * ff], wu[r, :], NT)

    def fill(out, quarter, low, high, extra=None):
        def step(i, carry):
            column = pl.multiple_of(low + i * LANE, LANE)
            total = term(quarter, column)
            if extra is not None:
                total = total + extra(column)
            out[:, pl.ds(column, LANE)] = total.astype(BF)
            return carry

        lax.fori_loop(0, (high - low) // LANE, step, 0)

    first, second = pl.ds(0, half), pl.ds(half, half)
    fill(far, up1(up1(t)), 0, part)
    f_right = links.start(far.at[:, first], far_in.at[:, first], right)
    f_left = links.start(far.at[:, second], far_in.at[:, second], left)
    g0.two()
    g1.two()
    fill(up_buf, up1(t), half, part)
    d_right = links.start(up_buf.at[:, second], sum_in.at[0, :, second], right)
    fill(down_buf, down1(t), 0, half)
    d_left = links.start(down_buf.at[:, first], sum_in.at[1, :, first], left)
    scores = [
        links.start(score, score_in.at[0], right),
        links.start(score, score_in.at[1], left),
        links.start(score, score_in.at[2], across),
    ]
    g0.three()
    g1.three()
    f_right.wait_recv()
    fill(up_buf, up1(t), 0, half, lambda k: far_in[:, pl.ds(k, LANE)].astype(F32))
    s_right = links.start(up_buf.at[:, first], sum_in.at[0, :, first], right)
    f_left.wait_recv()
    fill(down_buf, down1(t), half, part, lambda k: far_in[:, pl.ds(k, LANE)].astype(F32))
    s_left = links.start(down_buf.at[:, second], sum_in.at[1, :, second], left)
    g0.four()
    g1.four()
    for copy in scores:
        copy.wait_recv()
    total = jnp.zeros((rows, 1), F32)
    for ref in (score, score_in.at[0], score_in.at[1], score_in.at[2]):
        both = ref[...].astype(F32)
        total = total + (both[:, 0:1] + both[:, LANE // 2 : LANE // 2 + 1])
    padded = 16
    spread = jnp.where(
        (
            lax.div(lax.broadcasted_iota(jnp.int32, (slots * padded, rows), 0), padded) * cap
            + lax.rem(lax.broadcasted_iota(jnp.int32, (slots * padded, rows), 0), padded)
            == lax.broadcasted_iota(jnp.int32, (slots * padded, rows), 1)
        )
        & (
            lax.rem(lax.broadcasted_iota(jnp.int32, (slots * padded, rows), 0), padded) < cap
        ),
        1.0,
        0.0,
    ).astype(BF)
    back[:, :, pl.ds(part, LANE)] = (
        dot(spread, jnp.broadcast_to(total, (rows, LANE)).astype(BF))
        .astype(BF)
        .reshape(slots, padded, LANE)
    )
    for copy in (d_right, d_left, s_right, s_left):
        copy.wait_recv()

    def last(i, carry):
        column = pl.multiple_of(i * LANE, LANE)
        cols = pl.ds(column, LANE)
        total = term(t, column) + sum_in[0, :, cols].astype(F32) + sum_in[1, :, cols].astype(F32)
        own_buf[...] = total.astype(BF)
        back[:, :, cols] = dot(spread, own_buf[...]).astype(BF).reshape(slots, padded, LANE)
        return carry

    lax.fori_loop(0, part // LANE, last, 0)
    g0.five()
    g1.five()
    g0.six()
    g1.six()
    links.drain()


def weights_kernel(
    dims, owners, replicas, meta_all, cuts, acts, out, row_at, gate_at, xs, ds_, kept
):
    per, width, cap, top, ff = dims
    slots = RING * RING * CORES
    group_rows = cap * slots // RING
    line = per * slots // RING
    own = width // slots
    i = pl.program_id(0)
    slot = jnp.where(i < replicas, slots - replicas + i, i - replicas)

    @pl.when(i == 0)
    def _():
        ids = lax.broadcasted_iota(jnp.int32, (slots, 1), 0)
        for g in range(RING):
            row, gate, _ = entries(
                meta_all[pl.ds(g * line, line), :], ids, per, cap, top
            )
            row_at[g] = row
            gate_at[g] = gate

    for g in range(RING):
        chosen = picks(row_at[g, pl.ds(slot, 1), :], group_rows)
        weighed = chosen * gate_at[g, pl.ds(slot, 1), :]
        toks = pl.ds(g * line, line)
        rows = pl.ds(g * group_rows, group_rows)
        xs[rows, :] = dot(chosen.astype(BF), cuts[0, toks, :]).astype(BF)
        ds_[rows, :] = dot(weighed.astype(BF), cuts[1, toks, :]).astype(BF)
    in_grads = dot(xs[...], acts[0, :, 0 : 2 * ff], TN)
    down = dot(ds_[...], acts[0, :, 2 * ff :], TN)
    parts = (in_grads[:own, :ff], in_grads[:own, ff:], down[:own])

    @pl.when(i < replicas)
    def _():
        for k in range(3):
            kept[i, k] = parts[k]

    @pl.when(i >= replicas)
    def _():
        expert = i - replicas
        owned = owners[0] == expert
        for r in range(1, replicas):
            owned = owned | (owners[r] == expert)

        @pl.when(jnp.logical_not(owned))
        def _():
            for k in range(3):
                out[0, k] = parts[k].astype(BF)

        @pl.when(owned)
        def _():
            for k in range(3):
                total = parts[k]
                for r in range(replicas):
                    total = total + jnp.where(owners[r] == expert, kept[r, k], 0.0)
                out[0, k] = total.astype(BF)


def tokens_kernel(dims, meta, back, input_grads, gate_grads):
    per, width, cap, top, ff = dims
    slots = RING * RING * CORES
    part = width // RING
    padded = back.shape[1]
    ids = lax.broadcasted_iota(jnp.int32, (slots, 1), 0)
    row, _, turned = entries(meta[...], ids, per, cap, top)
    place = lax.broadcasted_iota(jnp.int32, (slots, padded, LANE), 1).astype(F32)
    chosen = jnp.where(row[:, None, :] == place, 1.0, 0.0)
    flat = chosen.reshape(slots * padded, LANE).astype(BF)
    for k in range(part // (2 * LANE)):
        cols = pl.ds(k * 2 * LANE, 2 * LANE)
        rows = back[:, :, cols].reshape(slots * padded, 2 * LANE)
        input_grads[:, cols] = dot(flat, rows, TN)[:per].astype(BF)
    score = back[:, :, pl.ds(part, LANE)].astype(F32)
    by_slot = jnp.sum(chosen * score, axis=1)
    for k in range(top):
        same = turned[k : k + 1] == ids.astype(F32)
        line = jnp.sum(jnp.where(same, by_slot, 0.0), axis=0, keepdims=True)
        gate_grads[pl.ds(k, 1), :] = line[:, :per]


def per_device(tokens, cotangent, gate_weights, route_slots, replica_owner, w_gate, w_up, w_down):
    slots = lax.axis_size("expert")
    per, width = tokens.shape
    top = route_slots.shape[1]
    cap = per * top * 3 // 2 // slots
    ff = w_gate.shape[2]
    rows = cap * slots
    part = width // RING
    padded = 16
    replicas = replica_owner.shape[0]
    experts = slots - replicas
    dims = (per, width, cap, top, ff)
    meta = jnp.concatenate(
        [
            route_slots.astype(BF),
            gate_weights,
            jnp.full((per, LANE - 2 * top), -1, BF),
        ],
        axis=1,
    )
    w_gate, w_up, w_down = w_gate[0], w_up[0], w_down[0]
    any_ = pl.BlockSpec(memory_space=pl.ANY)
    vmem = pl.BlockSpec(memory_space=pltpu.VMEM)
    line = per * slots // RING
    copies = 4 * GATHER_COPIES
    acts, score, cuts, meta_all = pl.pallas_call(
        functools.partial(dispatch_kernel, dims),
        name="dispatch",
        out_shape=(
            jax.ShapeDtypeStruct((rows, 3 * ff), BF),
            jax.ShapeDtypeStruct((rows, LANE), BF),
            jax.ShapeDtypeStruct((2, per * slots, 2 * LANE), BF),
            jax.ShapeDtypeStruct((per * slots, LANE), BF),
        ),
        in_specs=[any_] * 6,
        out_specs=(vmem,) * 4,
        scratch_shapes=[
            pltpu.VMEM((RING, RING, CORES, per, LANE + 2 * width), BF),
            pltpu.VMEM((width, ff), BF),
            pltpu.VMEM((width, ff), BF),
            pltpu.VMEM((width, ff), BF),
            pltpu.VMEM((rows, 512), BF),
            pltpu.VMEM((rows, ff), F32),
            pltpu.VMEM((rows, ff), F32),
            pltpu.VMEM((rows, ff), F32),
            pltpu.VMEM((RING, rows // RING, line), BF),
            pltpu.VMEM((rows, LANE), F32),
            pltpu.SemaphoreType.DMA((copies,)),
            pltpu.SemaphoreType.DMA((copies,)),
            pltpu.SemaphoreType.DMA((6,)),
        ],
        compiler_params=pltpu.CompilerParams(
            collective_id=0, has_side_effects=True, vmem_limit_bytes=56 * MIB
        ),
    )(tokens, cotangent, meta, w_gate, w_up, w_down)
    copies = 2 * GATHER_COPIES + 9
    acts_all, back = pl.pallas_call(
        functools.partial(return_kernel, dims),
        name="activations_out",
        out_shape=(
            jax.ShapeDtypeStruct((RING, RING, CORES, rows, 3 * ff), BF),
            jax.ShapeDtypeStruct((slots, padded, part + LANE), BF),
        ),
        in_specs=[any_, vmem, any_, any_],
        out_specs=(any_, vmem),
        scratch_shapes=[
            pltpu.VMEM((width, ff), BF),
            pltpu.VMEM((width, ff), BF),
            pltpu.VMEM((rows, 3 * ff), BF),
            pltpu.VMEM((rows, part), BF),
            pltpu.VMEM((rows, part), BF),
            pltpu.VMEM((rows, part), BF),
            pltpu.VMEM((rows, part), BF),
            pltpu.VMEM((2, rows, part), BF),
            pltpu.VMEM((rows, LANE), BF),
            pltpu.VMEM((3, rows, LANE), BF),
            pltpu.SemaphoreType.DMA((copies,)),
            pltpu.SemaphoreType.DMA((copies,)),
            pltpu.SemaphoreType.DMA((4,)),
        ],
        compiler_params=pltpu.CompilerParams(
            collective_id=1, has_side_effects=True, vmem_limit_bytes=56 * MIB
        ),
    )(acts, score, w_gate, w_up)
    returned = lax.all_to_all(back, "expert", 0, 0, tiled=True)
    own = width // slots
    expert_grads = pl.pallas_call(
        lambda owners, *refs: weights_kernel(dims, owners, replicas, *refs),
        name="weight_grads",
        out_shape=jax.ShapeDtypeStruct((experts, 3, own, ff), BF),
        grid_spec=pltpu.PrefetchScalarGridSpec(
            num_scalar_prefetch=1,
            grid=(slots,),
            in_specs=[
                pl.BlockSpec((per * slots, LANE), lambda i, o: (0, 0)),
                pl.BlockSpec((2, per * slots, 2 * LANE), lambda i, o: (0, 0, 0)),
                pl.BlockSpec(
                    (1, rows, 3 * ff),
                    lambda i, o: (jnp.where(i < replicas, experts + i, i - replicas), 0, 0),
                ),
            ],
            out_specs=pl.BlockSpec(
                (1, 3, own, ff), lambda i, o: (jnp.maximum(i - replicas, 0), 0, 0, 0)
            ),
            scratch_shapes=[
                pltpu.VMEM((RING, slots, line), F32),
                pltpu.VMEM((RING, slots, line), F32),
                pltpu.VMEM((rows, 2 * LANE), BF),
                pltpu.VMEM((rows, 2 * LANE), BF),
                pltpu.VMEM((replicas, 3, own, ff), F32),
            ],
        ),
        compiler_params=pltpu.CompilerParams(vmem_limit_bytes=40 * MIB),
        cost_estimate=pl.CostEstimate(
            flops=8_000_000_000, bytes_accessed=32_000_000, transcendentals=0
        ),
    )(replica_owner, meta_all, cuts, acts_all.reshape(slots, rows, 3 * ff))
    own_meta = jnp.concatenate([meta, jnp.full((LANE - per, LANE), -1, BF)], axis=0)
    input_grads, gate_grads = pl.pallas_call(
        functools.partial(tokens_kernel, dims),
        name="token_grads",
        out_shape=(
            jax.ShapeDtypeStruct((per, part), BF),
            jax.ShapeDtypeStruct((top, per), F32),
        ),
        in_specs=[vmem, vmem],
        out_specs=(vmem, vmem),
        compiler_params=pltpu.CompilerParams(vmem_limit_bytes=32 * MIB),
    )(own_meta, returned)
    return (
        input_grads,
        jnp.transpose(gate_grads.astype(BF)),
        jnp.transpose(expert_grads, (0, 2, 1, 3)),
    )


def solution(mesh):
    in_specs = (
        P("expert", None),
        P("expert", None),
        P("expert", None),
        P("expert", None),
        P(),
        P("expert", None, "tensor"),
        P("expert", None, "tensor"),
        P("expert", None, "tensor"),
    )
    out_specs = (P("expert", "tensor"), P("expert", None), P(None, "expert", None, "tensor"))
    return jax.shard_map(
        per_device, mesh=mesh, in_specs=in_specs, out_specs=out_specs, check_vma=False
    )
```

```python
import functools

import jax
import jax.numpy as jnp
from jax import lax
from jax.experimental import pallas as pl
from jax.experimental.pallas import tpu as pltpu
from jax.sharding import PartitionSpec as P

MESH = pl.DeviceIdType.MESH
BF = jnp.bfloat16
F32 = jnp.float32
LANE = 128
SHARED = 6
RING = 4
CORES = 2
MIB = 1 << 20
NT = (((1,), (1,)), ((), ()))
TN = (((0,), (0,)), ((), ()))


def dot(a, b, dims=None):
    if dims is None:
        return jnp.dot(a, b, preferred_element_type=F32)
    return lax.dot_general(a, b, dims, preferred_element_type=F32)


def up1(v):
    return lax.rem(v + 1, RING)


def down1(v):
    return lax.rem(v + RING - 1, RING)


def position():
    e = lax.axis_index("expert")
    t = lax.axis_index("tensor")
    return lax.div(e, CORES * RING), lax.rem(lax.div(e, CORES), RING), lax.rem(e, CORES), t


class Links:
    def __init__(self, send, recv):
        self.send, self.recv, self.count, self.started = send, recv, 0, []
        self.y, self.z, self.c, self.t = position()

    def to(self, y=None, z=None, c=None, t=None):
        y = self.y if y is None else y
        z = self.z if z is None else z
        c = self.c if c is None else c
        t = self.t if t is None else t
        return ((y * RING + z) * CORES + c, t)

    def start(self, src, dst, device):
        copy = pltpu.make_async_remote_copy(
            src_ref=src,
            dst_ref=dst,
            send_sem=self.send.at[self.count],
            recv_sem=self.recv.at[self.count],
            device_id=device,
            device_id_type=MESH,
        )
        self.count += 1
        copy.start()
        self.started.append(copy)
        return copy

    def greet(self, devices):
        barrier = pltpu.get_barrier_semaphore()
        for device in devices:
            pl.semaphore_signal(barrier, inc=1, device_id=device, device_id_type=MESH)
        pl.semaphore_wait(barrier, len(devices))

    def plane(self):
        return [
            self.to(y=up1(self.y)),
            self.to(y=down1(self.y)),
            self.to(z=up1(self.z)),
            self.to(z=down1(self.z)),
            self.to(c=1 - self.c),
        ]

    def drain(self):
        for copy in self.started:
            copy.wait_send()


class Gather:
    def __init__(self, links, at, y_first, handed=True):
        self.l, self.at, self.y_first, self.handed = links, at, y_first, handed
        self.first = links.y if y_first else links.z
        self.second = links.z if y_first else links.y

    def place(self, first, second, part=None):
        return self.at(first, second, part) if self.y_first else self.at(second, first, part)

    def along_first(self, v):
        return self.l.to(y=v) if self.y_first else self.l.to(z=v)

    def along_second(self, v):
        return self.l.to(z=v) if self.y_first else self.l.to(y=v)

    def copy(self, ref, device):
        return self.l.start(ref, ref, device)

    def hand_over(self, second):
        if self.handed:
            ref = self.place(slice(None), second)
            self.s.append(self.copy(ref, self.l.to(c=1 - self.l.c)))

    def lines(self):
        low, high = down1(self.second), up1(self.second)
        return [self.second, low, high, up1(high)]

    def one(self):
        own = self.place(self.first, self.second)
        self.m1 = self.copy(own, self.along_first(up1(self.first)))
        self.m2 = self.copy(own, self.along_first(down1(self.first)))

    def two(self):
        self.m1.wait_recv()
        self.m3 = self.copy(
            self.place(down1(self.first), self.second, 0), self.along_first(up1(self.first))
        )
        self.m2.wait_recv()
        self.m4 = self.copy(
            self.place(up1(self.first), self.second, 1), self.along_first(down1(self.first))
        )

    def three(self):
        self.m3.wait_recv()
        self.m4.wait_recv()
        line = self.place(slice(None), self.second)
        self.m5 = self.copy(line, self.along_second(up1(self.second)))
        self.m6 = self.copy(line, self.along_second(down1(self.second)))
        self.s = []
        self.hand_over(self.second)

    def four(self):
        low, high = down1(self.second), up1(self.second)
        self.m5.wait_recv()
        self.m7 = self.copy(self.place(slice(None), low, 0), self.along_second(high))
        self.hand_over(low)
        self.m6.wait_recv()
        self.m8 = self.copy(self.place(slice(None), high, 1), self.along_second(low))
        self.hand_over(high)

    def five(self):
        self.m7.wait_recv()
        self.m8.wait_recv()
        self.hand_over(up1(up1(self.second)))

    def six(self):
        for copy in self.s:
            copy.wait_recv()


GATHER_COPIES = 12


class Across:
    def __init__(self, links, at, whole):
        self.l, self.at, self.whole = links, at, whole

    def copy(self, ref, device):
        return self.l.start(ref, ref, device)

    def one(self):
        t = self.l.t
        self.m1 = self.copy(self.at(t), self.l.to(t=up1(t)))
        self.m2 = self.copy(self.at(t), self.l.to(t=down1(t)))

    def two(self):
        t = self.l.t
        self.m1.wait_recv()
        self.m3 = self.copy(self.at(down1(t), 0), self.l.to(t=up1(t)))
        self.m2.wait_recv()
        self.m4 = self.copy(self.at(up1(t), 1), self.l.to(t=down1(t)))

    def three(self):
        self.m3.wait_recv()
        self.m4.wait_recv()
        self.s = self.copy(self.whole, self.l.to(c=1 - self.l.c))

    def four(self):
        self.s.wait_recv()


ACROSS_COPIES = 5


def entries(meta, slot, per, cap, top):
    count = meta.shape[0]
    pick = (
        lax.broadcasted_iota(jnp.int32, (2 * top, LANE), 0)
        == lax.broadcasted_iota(jnp.int32, (2 * top, LANE), 1)
    ).astype(F32).astype(BF)
    turned = dot(pick, meta, NT)
    slot = slot.astype(F32)
    hit = jnp.zeros((slot.shape[0], count), F32)
    gate = jnp.zeros((slot.shape[0], count), F32)
    for k in range(top):
        same = turned[k : k + 1] == slot
        hit = hit + jnp.where(same, 1.0, 0.0)
        gate = gate + jnp.where(same, turned[top + k : top + k + 1], 0.0)
    earlier = lax.broadcasted_iota(jnp.int32, (count, count), 0)
    token = lax.broadcasted_iota(jnp.int32, (count, count), 1)
    before = jnp.where(
        (earlier < token) & (lax.div(earlier, per) == lax.div(token, per)), 1.0, 0.0
    ).astype(BF)
    place = dot(hit.astype(BF), before)
    block = lax.div(lax.broadcasted_iota(jnp.int32, hit.shape, 1), per).astype(F32)
    row = jnp.where(hit > 0.5, block * cap + place, -1.0)
    return row, gate, turned


def picks(row, group_rows):
    lines = lax.broadcasted_iota(jnp.int32, (group_rows, row.shape[1]), 0).astype(F32)
    return jnp.where(row == lines, 1.0, 0.0)


def dispatch_kernel(
    dims,
    tokens, cotangent, meta, w_gate, w_up, w_down,
    acts, score, cuts, meta_all,
    buf, wg, wu, wd, rows_buf, gate_acc, up_acc, down_acc, select, gate_rows,
    send, recv, local,
):
    per, width, cap, top, ff = dims
    slots = RING * RING * CORES
    group_rows = cap * slots // RING
    line = per * slots // RING
    links = Links(send, recv)
    y, z, c = links.y, links.z, links.c
    me = lax.axis_index("expert")
    x0, dy0 = LANE, LANE + width
    end = LANE + 2 * width
    loads = [
        pltpu.make_async_copy(meta, buf.at[y, z, c, :, pl.ds(0, LANE)], local.at[0]),
        pltpu.make_async_copy(tokens, buf.at[y, z, c, :, pl.ds(x0, width)], local.at[1]),
        pltpu.make_async_copy(cotangent, buf.at[y, z, c, :, pl.ds(dy0, width)], local.at[2]),
    ]
    weights = [
        pltpu.make_async_copy(w_gate, wg, local.at[3]),
        pltpu.make_async_copy(w_up, wu, local.at[4]),
        pltpu.make_async_copy(w_down, wd, local.at[5]),
    ]
    for copy in loads + weights:
        copy.start()
    for copy in loads:
        copy.wait()
    t = links.t
    links.greet(links.plane() + [links.to(t=up1(t)), links.to(t=down1(t))])

    def piece(start, size, y_first, handed=True):
        middle = size // (2 * LANE) * LANE
        spans = {None: (0, size), 0: (0, middle), 1: (middle, size - middle)}

        def at(yy, zz, part):
            low, count = spans[part]
            return buf.at[yy, zz, c, :, pl.ds(pl.multiple_of(start + low, LANE), count)]

        return Gather(links, at, y_first, handed)

    quarter = SHARED * LANE
    straight = width - RING * quarter
    half = straight // 2

    def across(first, gather):
        def ring(line):
            def at(owner, part=None):
                low, count = {
                    None: (0, quarter),
                    0: (0, quarter // 2),
                    1: (quarter // 2, quarter // 2),
                }[part]
                cols = pl.ds(pl.multiple_of(first + owner * quarter + low, LANE), count)
                if gather.y_first:
                    return buf.at[:, line, c, :, cols]
                return buf.at[line, :, c, :, cols]

            cols = pl.ds(first, RING * quarter)
            if gather.y_first:
                whole = buf.at[:, line, c, :, cols]
            else:
                whole = buf.at[line, :, c, :, cols]
            return Across(links, at, whole)

        return [ring(line) for line in gather.lines()]

    qx0, qdy0 = x0 + straight, dy0 + straight
    qa = piece(qx0 + t * quarter, quarter, True, False)
    qb = piece(qdy0 + t * quarter, quarter, False, False)
    xa, xb = across(qx0, qa), across(qdy0, qb)
    p0 = piece(0, x0 + half, True)
    p1 = piece(x0 + half, half, False)
    p2 = piece(dy0, half, True)
    p3 = piece(dy0 + half, half, False)
    qa.one()
    qb.one()
    qa.two()
    qb.two()
    p0.one()
    p1.one()
    qa.three()
    xa[0].one()
    qb.three()
    xb[0].one()
    p0.two()
    p1.two()
    qa.four()
    xa[1].one()
    xa[2].one()
    qb.four()
    p0.three()
    p1.three()
    qa.five()
    xa[3].one()
    qb.five()
    p2.one()
    p3.one()
    xa[0].two()
    xb[1].one()
    xb[2].one()
    p2.two()
    p3.two()
    xa[1].two()
    xa[2].two()
    xb[3].one()
    p0.four()
    p1.four()
    p2.three()
    p3.three()
    xa[3].two()
    xa[0].three()
    xb[0].two()
    p0.five()
    p1.five()
    xa[1].three()
    xa[2].three()
    xb[1].two()
    xb[2].two()
    p0.six()
    p1.six()

    for copy in weights:
        copy.wait()
    my_slot = jnp.full((8, 1), me, jnp.int32)
    for g in range(RING):
        part = buf[g, :, :, :, pl.ds(0, LANE)].reshape(line, LANE)
        meta_all[pl.ds(g * line, line), :] = part
        row, gate, _ = entries(part, my_slot, per, cap, top)
        chosen = picks(row[0:1], group_rows)
        select[g] = chosen.astype(BF)
        gate_rows[pl.ds(g * group_rows, group_rows), :] = jnp.broadcast_to(
            jnp.sum(chosen * gate[0:1], axis=1, keepdims=True), (group_rows, LANE)
        )

    chunk = 512

    def fill_rows(start):
        for g in range(RING):
            part = buf[g, :, :, :, pl.ds(start, chunk)].reshape(line, chunk)
            rows_buf[pl.ds(g * group_rows, group_rows), :] = dot(select[g], part).astype(BF)

    gate_acc[...] = jnp.zeros_like(gate_acc)
    up_acc[...] = jnp.zeros_like(up_acc)
    down_acc[...] = jnp.zeros_like(down_acc)

    def x_step(i, carry):
        off = pl.multiple_of(i * chunk, chunk)
        fill_rows(pl.multiple_of(x0 + i * chunk, LANE))
        gate_acc[...] += dot(rows_buf[...], wg[pl.ds(off, chunk), :])
        up_acc[...] += dot(rows_buf[...], wu[pl.ds(off, chunk), :])
        return carry

    def dy_step(i, carry):
        off = pl.multiple_of(i * chunk, chunk)
        fill_rows(pl.multiple_of(dy0 + i * chunk, LANE))
        down_acc[...] += dot(rows_buf[...], wd[pl.ds(off, chunk), :])
        return carry

    own = width // slots
    window = 3 * LANE
    low = jnp.minimum(lax.div(me * own, LANE) * LANE, width - window)
    shift = me * own - low
    move = jnp.where(
        lax.broadcasted_iota(jnp.int32, (window, 2 * LANE), 0)
        == lax.broadcasted_iota(jnp.int32, (window, 2 * LANE), 1) + shift,
        1.0,
        0.0,
    ).astype(BF)

    def cut(k, start):
        for g in range(RING):
            part = buf[g, :, :, :, pl.ds(pl.multiple_of(start + low, LANE), window)]
            cuts[k, pl.ds(g * line, line), :] = dot(part.reshape(line, window), move).astype(BF)

    strip = 32

    def silu_step(i, carry):
        r = pl.ds(pl.multiple_of(i * strip, strip), strip)
        gate_proj, up_proj = gate_acc[r, :], up_acc[r, :]
        sig = jax.nn.sigmoid(gate_proj)
        activated = gate_proj * sig
        acts[r, pl.ds(2 * ff, ff)] = (activated * up_proj).astype(BF)
        gate_acc[r, :] = up_proj * sig * (1.0 + gate_proj * (1.0 - sig))
        up_acc[r, :] = activated
        return carry

    def finish(i, carry):
        r = pl.ds(pl.multiple_of(i * strip, strip), strip)
        down_proj = down_acc[r, :]
        hidden_grad = gate_rows[r, 0:1] * down_proj
        acts[r, pl.ds(0, ff)] = (hidden_grad * gate_acc[r, :]).astype(BF)
        acts[r, pl.ds(ff, ff)] = (hidden_grad * up_acc[r, :]).astype(BF)
        hidden = acts[r, pl.ds(2 * ff, ff)].astype(F32)
        total = jnp.sum(hidden * down_proj, axis=1, keepdims=True)
        high = total.astype(BF)
        low_part = (total - high.astype(F32)).astype(BF)
        lanes = lax.broadcasted_iota(jnp.int32, (strip, LANE), 1)
        score[r, :] = jnp.where(
            lanes < LANE // 2, high.astype(F32), low_part.astype(F32)
        ).astype(BF)
        return carry

    steps, plain = width // chunk, straight // chunk
    strips = cap * slots // strip
    lax.fori_loop(0, plain, x_step, 0)
    p2.four()
    p3.four()
    xa[3].three()
    xb[0].three()
    xb[3].two()
    for ring in xa:
        ring.four()
    lax.fori_loop(plain, steps, x_step, 0)
    xb[1].three()
    xb[2].three()
    cut(0, x0)
    lax.fori_loop(0, strips, silu_step, 0)
    p2.five()
    p3.five()
    xb[3].three()
    p2.six()
    p3.six()
    lax.fori_loop(0, plain, dy_step, 0)
    for ring in xb:
        ring.four()
    lax.fori_loop(plain, steps, dy_step, 0)
    cut(1, dy0)
    lax.fori_loop(0, strips, finish, 0)
    links.drain()


def return_kernel(
    dims,
    acts, score, meta_all, cuts, w_gate, w_up,
    acts_all, turned_all, back,
    held_all, wg, wu, a, far, up_buf, down_buf, far_in, sum_in, own_buf, score_in,
    row_at, gate_at, rows_buf, turned,
    send, recv, local, out_sem,
):
    per, width, cap, top, ff = dims
    slots = RING * RING * CORES
    rows = cap * slots
    part = width // RING
    half = part // 2
    links = Links(send, recv)
    y, z, c, t = links.y, links.z, links.c, links.t
    own = pltpu.make_async_copy(acts, held_all.at[y, z, c], local.at[0])
    held = pltpu.make_async_copy(acts, a, local.at[1])
    weights = [
        pltpu.make_async_copy(w_gate, wg, local.at[2]),
        pltpu.make_async_copy(w_up, wu, local.at[3]),
    ]
    for copy in [own, held] + weights:
        copy.start()
    own.wait()
    right, left, across = links.to(t=up1(t)), links.to(t=down1(t)), links.to(t=up1(up1(t)))
    links.greet(links.plane() + [right, left, across])

    def piece(start, stop, y_first):
        middle = (start + stop) // 2
        spans = {None: (start, stop), 0: (start, middle), 1: (middle, stop)}

        def at(yy, zz, which):
            low, high = spans[which]
            return held_all.at[yy, zz, c, pl.ds(low, high - low), :]

        return Gather(links, at, y_first)

    outs = []

    def copy_out(gather, index, core):
        line = gather.lines()[index]
        r = pl.ds(0, rows // 2) if gather.y_first else pl.ds(rows // 2, rows // 2)
        if gather.y_first:
            src, dst = held_all.at[:, line, core, r, :], acts_all.at[:, line, core, r, :]
        else:
            src, dst = held_all.at[line, :, core, r, :], acts_all.at[line, :, core, r, :]
        outs.append(pltpu.make_async_copy(src, dst, out_sem.at[len(outs)]))
        outs[-1].start()

    group_rows = rows // RING
    line_tokens = per * slots // RING
    width_own = width // slots

    def place_rows():
        ids = lax.broadcasted_iota(jnp.int32, (slots, 1), 0)
        for g in range(RING):
            row, gate, _ = entries(
                meta_all[pl.ds(g * line_tokens, line_tokens), :], ids, per, cap, top
            )
            row_at[g] = row
            gate_at[g] = gate

    several = 4

    def turn_step(i, carry):
        for g in range(RING):
            toks = pl.ds(g * line_tokens, line_tokens)
            chosen, weighed = [], []
            for j in range(several):
                slot = i * several + j
                pick = picks(row_at[g, pl.ds(slot, 1), :], group_rows)
                chosen.append(pick.astype(BF))
                weighed.append((pick * gate_at[g, pl.ds(slot, 1), :]).astype(BF))
            for k, lhs in enumerate((chosen, weighed)):
                found = dot(jnp.concatenate(lhs, axis=0), cuts[k, toks, :])
                for j in range(several):
                    rows_buf[j, k, pl.ds(g * group_rows, group_rows), :] = found[
                        j * group_rows : (j + 1) * group_rows
                    ].astype(BF)
        for j in range(several):
            for k in range(2):
                turned[i * several + j, k] = jnp.transpose(rows_buf[j, k])[:width_own]
        return carry

    g0 = piece(0, rows // 2, True)
    g1 = piece(rows // 2, rows, False)
    g0.one()
    g1.one()
    held.wait()
    for copy in weights:
        copy.wait()

    def term(quarter, column):
        r = pl.ds(pl.multiple_of(quarter * part + column, LANE), LANE)
        return dot(a[:, 0:ff], wg[r, :], NT) + dot(a[:, ff : 2 * ff], wu[r, :], NT)

    def fill(out, quarter, low, high, extra=None):
        def step(i, carry):
            column = pl.multiple_of(low + i * LANE, LANE)
            total = term(quarter, column)
            if extra is not None:
                total = total + extra(column)
            out[:, pl.ds(column, LANE)] = total.astype(BF)
            return carry

        lax.fori_loop(0, (high - low) // LANE, step, 0)

    first, second = pl.ds(0, half), pl.ds(half, half)
    fill(far, up1(up1(t)), 0, part)
    f_right = links.start(far.at[:, first], far_in.at[:, first], right)
    f_left = links.start(far.at[:, second], far_in.at[:, second], left)
    g0.two()
    g1.two()
    fill(up_buf, up1(t), half, part)
    d_right = links.start(up_buf.at[:, second], sum_in.at[0, :, second], right)
    fill(down_buf, down1(t), 0, half)
    d_left = links.start(down_buf.at[:, first], sum_in.at[1, :, first], left)
    scores = [
        links.start(score, score_in.at[0], right),
        links.start(score, score_in.at[1], left),
        links.start(score, score_in.at[2], across),
    ]
    place_rows()
    g0.three()
    g1.three()
    copy_out(g0, 0, c)
    copy_out(g1, 0, c)
    f_right.wait_recv()
    fill(up_buf, up1(t), 0, half, lambda k: far_in[:, pl.ds(k, LANE)].astype(F32))
    s_right = links.start(up_buf.at[:, first], sum_in.at[0, :, first], right)
    f_left.wait_recv()
    fill(down_buf, down1(t), half, part, lambda k: far_in[:, pl.ds(k, LANE)].astype(F32))
    s_left = links.start(down_buf.at[:, second], sum_in.at[1, :, second], left)
    lax.fori_loop(0, slots // several, turn_step, 0)
    turned_out = pltpu.make_async_copy(turned, turned_all, local.at[4])
    turned_out.start()
    g0.four()
    g1.four()
    for gather in (g0, g1):
        copy_out(gather, 1, c)
        copy_out(gather, 2, c)
    for copy in scores:
        copy.wait_recv()
    total = jnp.zeros((rows, 1), F32)
    for ref in (score, score_in.at[0], score_in.at[1], score_in.at[2]):
        both = ref[...].astype(F32)
        total = total + (both[:, 0:1] + both[:, LANE // 2 : LANE // 2 + 1])
    padded = 16
    spread = jnp.where(
        (
            lax.div(lax.broadcasted_iota(jnp.int32, (slots * padded, rows), 0), padded) * cap
            + lax.rem(lax.broadcasted_iota(jnp.int32, (slots * padded, rows), 0), padded)
            == lax.broadcasted_iota(jnp.int32, (slots * padded, rows), 1)
        )
        & (
            lax.rem(lax.broadcasted_iota(jnp.int32, (slots * padded, rows), 0), padded) < cap
        ),
        1.0,
        0.0,
    ).astype(BF)
    back[:, :, pl.ds(part, LANE)] = (
        dot(spread, jnp.broadcast_to(total, (rows, LANE)).astype(BF))
        .astype(BF)
        .reshape(slots, padded, LANE)
    )
    for copy in (d_right, d_left, s_right, s_left):
        copy.wait_recv()

    def last(i, carry):
        column = pl.multiple_of(i * LANE, LANE)
        cols = pl.ds(column, LANE)
        total = term(t, column) + sum_in[0, :, cols].astype(F32) + sum_in[1, :, cols].astype(F32)
        own_buf[...] = total.astype(BF)
        back[:, :, cols] = dot(spread, own_buf[...]).astype(BF).reshape(slots, padded, LANE)
        return carry

    lax.fori_loop(0, part // LANE, last, 0)
    g0.five()
    g1.five()
    for gather in (g0, g1):
        copy_out(gather, 3, c)
    for gather in (g0, g1):
        gather.six()
        for index in range(RING):
            copy_out(gather, index, 1 - c)
    links.drain()
    turned_out.wait()
    for copy in outs:
        copy.wait()


def weights_kernel(dims, owners, replicas, turned, acts, out, kept):
    ff = dims[-1]
    i = pl.program_id(0)

    def parts(j):
        in_grads = dot(turned[j, 0], acts[j, :, 0 : 2 * ff])
        down = dot(turned[j, 1], acts[j, :, 2 * ff :])
        return in_grads[:, :ff], in_grads[:, ff:], down

    @pl.when(i == 0)
    def _():
        for j in range(replicas):
            for k, part in enumerate(parts(j)):
                kept[j, k] = part

    @pl.when(i > 0)
    def _():
        for j in range(replicas):
            for k, part in enumerate(parts(j)):
                out[j, k] = part.astype(BF)
            expert = (i - 1) * replicas + j
            owned = owners[0] == expert
            for r in range(1, replicas):
                owned = owned | (owners[r] == expert)

            @pl.when(owned)
            def _():
                for k in range(3):
                    total = out[j, k].astype(F32)
                    for r in range(replicas):
                        total = total + jnp.where(owners[r] == expert, kept[r, k], 0.0)
                    out[j, k] = total.astype(BF)


def tokens_kernel(dims, meta, back, input_grads, gate_grads):
    per, width, cap, top, ff = dims
    slots = RING * RING * CORES
    part = width // RING
    padded = back.shape[1]
    ids = lax.broadcasted_iota(jnp.int32, (slots, 1), 0)
    row, _, turned = entries(meta[...], ids, per, cap, top)
    place = lax.broadcasted_iota(jnp.int32, (slots, padded, LANE), 1).astype(F32)
    chosen = jnp.where(row[:, None, :] == place, 1.0, 0.0)
    flat = chosen.reshape(slots * padded, LANE).astype(BF)
    for k in range(part // (2 * LANE)):
        cols = pl.ds(k * 2 * LANE, 2 * LANE)
        rows = back[:, :, cols].reshape(slots * padded, 2 * LANE)
        input_grads[:, cols] = dot(flat, rows, TN)[:per].astype(BF)
    score = back[:, :, pl.ds(part, LANE)].astype(F32)
    by_slot = jnp.sum(chosen * score, axis=1)
    for k in range(top):
        same = turned[k : k + 1] == ids.astype(F32)
        line = jnp.sum(jnp.where(same, by_slot, 0.0), axis=0, keepdims=True)
        gate_grads[pl.ds(k, 1), :] = line[:, :per]


def per_device(tokens, cotangent, gate_weights, route_slots, replica_owner, w_gate, w_up, w_down):
    slots = lax.axis_size("expert")
    per, width = tokens.shape
    top = route_slots.shape[1]
    cap = per * top * 3 // 2 // slots
    ff = w_gate.shape[2]
    rows = cap * slots
    part = width // RING
    padded = 16
    replicas = replica_owner.shape[0]
    experts = slots - replicas
    dims = (per, width, cap, top, ff)
    meta = jnp.concatenate(
        [
            route_slots.astype(BF),
            gate_weights,
            jnp.full((per, LANE - 2 * top), -1, BF),
        ],
        axis=1,
    )
    w_gate, w_up, w_down = w_gate[0], w_up[0], w_down[0]
    any_ = pl.BlockSpec(memory_space=pl.ANY)
    vmem = pl.BlockSpec(memory_space=pltpu.VMEM)
    line = per * slots // RING
    copies = 4 * GATHER_COPIES + 2 * (GATHER_COPIES - 4) + 8 * ACROSS_COPIES
    acts, score, cuts, meta_all = pl.pallas_call(
        functools.partial(dispatch_kernel, dims),
        name="dispatch",
        out_shape=(
            jax.ShapeDtypeStruct((rows, 3 * ff), BF),
            jax.ShapeDtypeStruct((rows, LANE), BF),
            jax.ShapeDtypeStruct((2, per * slots, 2 * LANE), BF),
            jax.ShapeDtypeStruct((per * slots, LANE), BF),
        ),
        in_specs=[any_] * 6,
        out_specs=(vmem,) * 4,
        scratch_shapes=[
            pltpu.VMEM((RING, RING, CORES, per, LANE + 2 * width), BF),
            pltpu.VMEM((width, ff), BF),
            pltpu.VMEM((width, ff), BF),
            pltpu.VMEM((width, ff), BF),
            pltpu.VMEM((rows, 512), BF),
            pltpu.VMEM((rows, ff), F32),
            pltpu.VMEM((rows, ff), F32),
            pltpu.VMEM((rows, ff), F32),
            pltpu.VMEM((RING, rows // RING, line), BF),
            pltpu.VMEM((rows, LANE), F32),
            pltpu.SemaphoreType.DMA((copies,)),
            pltpu.SemaphoreType.DMA((copies,)),
            pltpu.SemaphoreType.DMA((6,)),
        ],
        compiler_params=pltpu.CompilerParams(
            collective_id=0, has_side_effects=True, vmem_limit_bytes=56 * MIB
        ),
    )(tokens, cotangent, meta, w_gate, w_up, w_down)
    copies = 2 * GATHER_COPIES + 9
    own = width // slots
    acts_all, turned_all, back = pl.pallas_call(
        functools.partial(return_kernel, dims),
        name="activations_out",
        out_shape=(
            jax.ShapeDtypeStruct((RING, RING, CORES, rows, 3 * ff), BF),
            jax.ShapeDtypeStruct((slots, 2, own, rows), BF),
            jax.ShapeDtypeStruct((slots, padded, part + LANE), BF),
        ),
        in_specs=[any_, vmem, vmem, vmem, any_, any_],
        out_specs=(any_, any_, vmem),
        scratch_shapes=[
            pltpu.VMEM((RING, RING, CORES, rows, 3 * ff), BF),
            pltpu.VMEM((width, ff), BF),
            pltpu.VMEM((width, ff), BF),
            pltpu.VMEM((rows, 3 * ff), BF),
            pltpu.VMEM((rows, part), BF),
            pltpu.VMEM((rows, part), BF),
            pltpu.VMEM((rows, part), BF),
            pltpu.VMEM((rows, part), BF),
            pltpu.VMEM((2, rows, part), BF),
            pltpu.VMEM((rows, LANE), BF),
            pltpu.VMEM((3, rows, LANE), BF),
            pltpu.VMEM((RING, slots, line), F32),
            pltpu.VMEM((RING, slots, line), F32),
            pltpu.VMEM((4, 2, rows, 2 * LANE), BF),
            pltpu.VMEM((slots, 2, own, rows), BF),
            pltpu.SemaphoreType.DMA((copies,)),
            pltpu.SemaphoreType.DMA((copies,)),
            pltpu.SemaphoreType.DMA((5,)),
            pltpu.SemaphoreType.DMA((4 * RING,)),
        ],
        compiler_params=pltpu.CompilerParams(
            collective_id=1, has_side_effects=True, vmem_limit_bytes=60 * MIB
        ),
    )(acts, score, meta_all, cuts, w_gate, w_up)
    returned = lax.all_to_all(back, "expert", 0, 0, tiled=True)

    steps = slots // replicas

    def from_slot(i):
        return jnp.where(i == 0, steps - 1, i - 1)

    expert_grads = pl.pallas_call(
        lambda owners, *refs: weights_kernel(dims, owners, replicas, *refs),
        name="weight_grads",
        out_shape=jax.ShapeDtypeStruct((experts, 3, own, ff), BF),
        grid_spec=pltpu.PrefetchScalarGridSpec(
            num_scalar_prefetch=1,
            grid=(steps,),
            in_specs=[
                pl.BlockSpec((replicas, 2, own, rows), lambda i, o: (from_slot(i), 0, 0, 0)),
                pl.BlockSpec((replicas, rows, 3 * ff), lambda i, o: (from_slot(i), 0, 0)),
            ],
            out_specs=pl.BlockSpec(
                (replicas, 3, own, ff), lambda i, o: (jnp.maximum(i - 1, 0), 0, 0, 0)
            ),
            scratch_shapes=[pltpu.VMEM((replicas, 3, own, ff), F32)],
        ),
        compiler_params=pltpu.CompilerParams(vmem_limit_bytes=40 * MIB),
        cost_estimate=pl.CostEstimate(
            flops=5_000_000_000, bytes_accessed=40_000_000, transcendentals=0
        ),
    )(replica_owner, turned_all, acts_all.reshape(slots, rows, 3 * ff))
    own_meta = jnp.concatenate([meta, jnp.full((LANE - per, LANE), -1, BF)], axis=0)
    input_grads, gate_grads = pl.pallas_call(
        functools.partial(tokens_kernel, dims),
        name="token_grads",
        out_shape=(
            jax.ShapeDtypeStruct((per, part), BF),
            jax.ShapeDtypeStruct((top, per), F32),
        ),
        in_specs=[vmem, vmem],
        out_specs=(vmem, vmem),
        compiler_params=pltpu.CompilerParams(vmem_limit_bytes=32 * MIB),
    )(own_meta, returned)
    return (
        input_grads,
        jnp.transpose(gate_grads.astype(BF)),
        jnp.transpose(expert_grads, (0, 2, 1, 3)),
    )


def solution(mesh):
    in_specs = (
        P("expert", None),
        P("expert", None),
        P("expert", None),
        P("expert", None),
        P(),
        P("expert", None, "tensor"),
        P("expert", None, "tensor"),
        P("expert", None, "tensor"),
    )
    out_specs = (P("expert", "tensor"), P("expert", None), P(None, "expert", None, "tensor"))
    return jax.shard_map(
        per_device, mesh=mesh, in_specs=in_specs, out_specs=out_specs, check_vma=False
    )
```

```python
import functools

import jax
import jax.numpy as jnp
from jax import lax
from jax.experimental import pallas as pl
from jax.experimental.pallas import tpu as pltpu
from jax.sharding import PartitionSpec as P

MESH = pl.DeviceIdType.MESH
BF = jnp.bfloat16
F32 = jnp.float32
LANE = 128
SHARED = 6
RING = 4
CORES = 2
MIB = 1 << 20
NT = (((1,), (1,)), ((), ()))
TN = (((0,), (0,)), ((), ()))


def dot(a, b, dims=None):
    if dims is None:
        return jnp.dot(a, b, preferred_element_type=F32)
    return lax.dot_general(a, b, dims, preferred_element_type=F32)


def up1(v):
    return lax.rem(v + 1, RING)


def down1(v):
    return lax.rem(v + RING - 1, RING)


def position():
    e = lax.axis_index("expert")
    t = lax.axis_index("tensor")
    return lax.div(e, CORES * RING), lax.rem(lax.div(e, CORES), RING), lax.rem(e, CORES), t


class Links:
    def __init__(self, send, recv):
        self.send, self.recv, self.count, self.started = send, recv, 0, []
        self.y, self.z, self.c, self.t = position()

    def to(self, y=None, z=None, c=None, t=None):
        y = self.y if y is None else y
        z = self.z if z is None else z
        c = self.c if c is None else c
        t = self.t if t is None else t
        return ((y * RING + z) * CORES + c, t)

    def start(self, src, dst, device):
        copy = pltpu.make_async_remote_copy(
            src_ref=src,
            dst_ref=dst,
            send_sem=self.send.at[self.count],
            recv_sem=self.recv.at[self.count],
            device_id=device,
            device_id_type=MESH,
        )
        self.count += 1
        copy.start()
        self.started.append(copy)
        return copy

    def greet(self, devices):
        barrier = pltpu.get_barrier_semaphore()
        for device in devices:
            pl.semaphore_signal(barrier, inc=1, device_id=device, device_id_type=MESH)
        pl.semaphore_wait(barrier, len(devices))

    def plane(self):
        return [
            self.to(y=up1(self.y)),
            self.to(y=down1(self.y)),
            self.to(z=up1(self.z)),
            self.to(z=down1(self.z)),
            self.to(c=1 - self.c),
        ]

    def drain(self):
        for copy in self.started:
            copy.wait_send()


class Gather:
    def __init__(self, links, at, y_first, handed=True):
        self.l, self.at, self.y_first, self.handed = links, at, y_first, handed
        self.first = links.y if y_first else links.z
        self.second = links.z if y_first else links.y

    def place(self, first, second, part=None):
        return self.at(first, second, part) if self.y_first else self.at(second, first, part)

    def along_first(self, v):
        return self.l.to(y=v) if self.y_first else self.l.to(z=v)

    def along_second(self, v):
        return self.l.to(z=v) if self.y_first else self.l.to(y=v)

    def copy(self, ref, device):
        return self.l.start(ref, ref, device)

    def hand_over(self, second):
        if self.handed:
            ref = self.place(slice(None), second)
            self.s.append(self.copy(ref, self.l.to(c=1 - self.l.c)))

    def lines(self):
        low, high = down1(self.second), up1(self.second)
        return [self.second, low, high, up1(high)]

    def one(self):
        own = self.place(self.first, self.second)
        self.m1 = self.copy(own, self.along_first(up1(self.first)))
        self.m2 = self.copy(own, self.along_first(down1(self.first)))

    def two(self):
        self.m1.wait_recv()
        self.m3 = self.copy(
            self.place(down1(self.first), self.second, 0), self.along_first(up1(self.first))
        )
        self.m2.wait_recv()
        self.m4 = self.copy(
            self.place(up1(self.first), self.second, 1), self.along_first(down1(self.first))
        )

    def three(self):
        self.m3.wait_recv()
        self.m4.wait_recv()
        line = self.place(slice(None), self.second)
        self.m5 = self.copy(line, self.along_second(up1(self.second)))
        self.m6 = self.copy(line, self.along_second(down1(self.second)))
        self.s = []
        self.hand_over(self.second)

    def four(self):
        low, high = down1(self.second), up1(self.second)
        self.m5.wait_recv()
        self.m7 = self.copy(self.place(slice(None), low, 0), self.along_second(high))
        self.hand_over(low)
        self.m6.wait_recv()
        self.m8 = self.copy(self.place(slice(None), high, 1), self.along_second(low))
        self.hand_over(high)

    def five(self):
        self.m7.wait_recv()
        self.m8.wait_recv()
        self.hand_over(up1(up1(self.second)))

    def six(self):
        for copy in self.s:
            copy.wait_recv()


GATHER_COPIES = 12


class Across:
    def __init__(self, links, at, whole):
        self.l, self.at, self.whole = links, at, whole

    def copy(self, ref, device):
        return self.l.start(ref, ref, device)

    def one(self):
        t = self.l.t
        self.m1 = self.copy(self.at(t), self.l.to(t=up1(t)))
        self.m2 = self.copy(self.at(t), self.l.to(t=down1(t)))

    def two(self):
        t = self.l.t
        self.m1.wait_recv()
        self.m3 = self.copy(self.at(down1(t), 0), self.l.to(t=up1(t)))
        self.m2.wait_recv()
        self.m4 = self.copy(self.at(up1(t), 1), self.l.to(t=down1(t)))

    def three(self):
        self.m3.wait_recv()
        self.m4.wait_recv()
        self.s = self.copy(self.whole, self.l.to(c=1 - self.l.c))

    def four(self):
        self.s.wait_recv()


ACROSS_COPIES = 5


class RingSum:
    def __init__(self, links, axis, at, far, sums, low, first, second):
        self.l, self.axis, self.at, self.far, self.sums = links, axis, at, far, sums
        self.me = getattr(links, axis)
        self.high, self.down = up1(self.me), down1(self.me)
        self.low, self.first, self.second = low, first, second

    def to(self, v):
        return self.l.to(**{self.axis: v})

    def part(self, v, k):
        if k == 0:
            return self.at(v, self.low, self.first)
        return self.at(v, self.low + self.first, self.second)

    def sum_part(self, side, k):
        low, count = (0, self.first) if k == 0 else (self.first, self.second)
        return self.sums(side, low, count)

    def one(self):
        across, start = up1(self.high), self.l.start
        high, down = self.to(self.high), self.to(self.down)
        self.f0 = start(self.part(across, 0), self.far(0, self.first), high)
        self.f1 = start(self.part(across, 1), self.far(1, self.second), down)
        self.d0 = start(self.part(self.high, 1), self.sum_part(0, 1), high)
        self.d1 = start(self.part(self.down, 0), self.sum_part(1, 0), down)

    def two(self):
        self.f0.wait_recv()
        ref = self.part(self.high, 0)
        ref[...] = (ref[...].astype(F32) + self.far(0, self.first)[...].astype(F32)).astype(BF)
        self.s0 = self.l.start(ref, self.sum_part(0, 0), self.to(self.high))
        self.f1.wait_recv()
        ref = self.part(self.down, 1)
        ref[...] = (ref[...].astype(F32) + self.far(1, self.second)[...].astype(F32)).astype(BF)
        self.s1 = self.l.start(ref, self.sum_part(1, 1), self.to(self.down))

    def three(self, put):
        for copy in (self.d0, self.d1, self.s0, self.s1):
            copy.wait_recv()
        for k in range(2):
            total = self.part(self.me, k)[...].astype(F32)
            for side in range(2):
                total = total + self.sum_part(side, k)[...].astype(F32)
            put(0 if k == 0 else self.first, total.astype(BF))


RING_COPIES = 6


def entries(meta, slot, per, cap, top):
    count = meta.shape[0]
    pick = (
        lax.broadcasted_iota(jnp.int32, (2 * top, LANE), 0)
        == lax.broadcasted_iota(jnp.int32, (2 * top, LANE), 1)
    ).astype(F32).astype(BF)
    turned = dot(pick, meta, NT)
    slot = slot.astype(F32)
    hit = jnp.zeros((slot.shape[0], count), F32)
    gate = jnp.zeros((slot.shape[0], count), F32)
    for k in range(top):
        same = turned[k : k + 1] == slot
        hit = hit + jnp.where(same, 1.0, 0.0)
        gate = gate + jnp.where(same, turned[top + k : top + k + 1], 0.0)
    earlier = lax.broadcasted_iota(jnp.int32, (count, count), 0)
    token = lax.broadcasted_iota(jnp.int32, (count, count), 1)
    before = jnp.where(
        (earlier < token) & (lax.div(earlier, per) == lax.div(token, per)), 1.0, 0.0
    ).astype(BF)
    place = dot(hit.astype(BF), before)
    block = lax.div(lax.broadcasted_iota(jnp.int32, hit.shape, 1), per).astype(F32)
    row = jnp.where(hit > 0.5, block * cap + place, -1.0)
    return row, gate, turned


def picks(row, group_rows):
    lines = lax.broadcasted_iota(jnp.int32, (group_rows, row.shape[1]), 0).astype(F32)
    return jnp.where(row == lines, 1.0, 0.0)


def dispatch_kernel(
    dims,
    tokens, cotangent, meta, w_gate, w_up, w_down,
    acts, score, cuts, meta_all,
    buf, wg, wu, wd, rows_buf, gate_acc, up_acc, down_acc, select, gate_rows,
    send, recv, local,
):
    per, width, cap, top, ff = dims
    slots = RING * RING * CORES
    group_rows = cap * slots // RING
    line = per * slots // RING
    links = Links(send, recv)
    y, z, c = links.y, links.z, links.c
    me = lax.axis_index("expert")
    x0, dy0 = LANE, LANE + width
    end = LANE + 2 * width
    loads = [
        pltpu.make_async_copy(meta, buf.at[y, z, c, :, pl.ds(0, LANE)], local.at[0]),
        pltpu.make_async_copy(tokens, buf.at[y, z, c, :, pl.ds(x0, width)], local.at[1]),
        pltpu.make_async_copy(cotangent, buf.at[y, z, c, :, pl.ds(dy0, width)], local.at[2]),
    ]
    weights = [
        pltpu.make_async_copy(w_gate, wg, local.at[3]),
        pltpu.make_async_copy(w_up, wu, local.at[4]),
        pltpu.make_async_copy(w_down, wd, local.at[5]),
    ]
    for copy in loads + weights:
        copy.start()
    for copy in loads:
        copy.wait()
    t = links.t
    links.greet(links.plane() + [links.to(t=up1(t)), links.to(t=down1(t))])

    def piece(start, size, y_first, handed=True):
        middle = size // (2 * LANE) * LANE
        spans = {None: (0, size), 0: (0, middle), 1: (middle, size - middle)}

        def at(yy, zz, part):
            low, count = spans[part]
            return buf.at[yy, zz, c, :, pl.ds(pl.multiple_of(start + low, LANE), count)]

        return Gather(links, at, y_first, handed)

    quarter = SHARED * LANE
    straight = width - RING * quarter

    def across(first, gather):
        def ring(line):
            def at(owner, part=None):
                low, count = {
                    None: (0, quarter),
                    0: (0, quarter // (2 * LANE) * LANE),
                    1: (quarter // (2 * LANE) * LANE, quarter - quarter // (2 * LANE) * LANE),
                }[part]
                cols = pl.ds(pl.multiple_of(first + owner * quarter + low, LANE), count)
                if gather.y_first:
                    return buf.at[:, line, c, :, cols]
                return buf.at[line, :, c, :, cols]

            cols = pl.ds(first, RING * quarter)
            if gather.y_first:
                whole = buf.at[:, line, c, :, cols]
            else:
                whole = buf.at[line, :, c, :, cols]
            return Across(links, at, whole)

        return [ring(line) for line in gather.lines()]

    qx0, qdy0 = x0 + straight, dy0 + straight
    qa = piece(qx0 + t * quarter, quarter, True, False)
    qb = piece(qdy0 + t * quarter, quarter, False, False)
    xa, xb = across(qx0, qa), across(qdy0, qb)
    half = straight // (2 * LANE) * LANE
    p0 = piece(0, x0 + half, True)
    p1 = piece(x0 + half, straight - half, False)
    p2 = piece(dy0, half, True)
    p3 = piece(dy0 + half, straight - half, False)
    qa.one()
    qb.one()
    qa.two()
    qb.two()
    p0.one()
    p1.one()
    qa.three()
    xa[0].one()
    qb.three()
    xb[0].one()
    p0.two()
    p1.two()
    qa.four()
    xa[1].one()
    xa[2].one()
    qb.four()
    p0.three()
    p1.three()
    qa.five()
    xa[3].one()
    qb.five()
    p2.one()
    p3.one()
    xa[0].two()
    xb[1].one()
    xb[2].one()
    p2.two()
    p3.two()
    xa[1].two()
    xa[2].two()
    xb[3].one()
    p0.four()
    p1.four()
    p2.three()
    p3.three()
    xa[3].two()
    xa[0].three()
    xb[0].two()
    p0.five()
    p1.five()
    xa[1].three()
    xa[2].three()
    xb[1].two()
    xb[2].two()
    p0.six()
    p1.six()

    for copy in weights:
        copy.wait()
    my_slot = jnp.full((8, 1), me, jnp.int32)
    for g in range(RING):
        part = buf[g, :, :, :, pl.ds(0, LANE)].reshape(line, LANE)
        meta_all[pl.ds(g * line, line), :] = part
        row, gate, _ = entries(part, my_slot, per, cap, top)
        chosen = picks(row[0:1], group_rows)
        select[g] = chosen.astype(BF)
        gate_rows[pl.ds(g * group_rows, group_rows), :] = jnp.broadcast_to(
            jnp.sum(chosen * gate[0:1], axis=1, keepdims=True), (group_rows, LANE)
        )

    chunk = 512

    def fill_rows(start):
        for g in range(RING):
            part = buf[g, :, :, :, pl.ds(start, chunk)].reshape(line, chunk)
            rows_buf[pl.ds(g * group_rows, group_rows), :] = dot(select[g], part).astype(BF)

    gate_acc[...] = jnp.zeros_like(gate_acc)
    up_acc[...] = jnp.zeros_like(up_acc)
    down_acc[...] = jnp.zeros_like(down_acc)

    def x_step(i, carry):
        off = pl.multiple_of(i * chunk, chunk)
        fill_rows(pl.multiple_of(x0 + i * chunk, LANE))
        gate_acc[...] += dot(rows_buf[...], wg[pl.ds(off, chunk), :])
        up_acc[...] += dot(rows_buf[...], wu[pl.ds(off, chunk), :])
        return carry

    def dy_step(i, carry):
        off = pl.multiple_of(i * chunk, chunk)
        fill_rows(pl.multiple_of(dy0 + i * chunk, LANE))
        down_acc[...] += dot(rows_buf[...], wd[pl.ds(off, chunk), :])
        return carry

    own = width // slots
    window = 3 * LANE
    low = jnp.minimum(lax.div(me * own, LANE) * LANE, width - window)
    shift = me * own - low
    move = jnp.where(
        lax.broadcasted_iota(jnp.int32, (window, 2 * LANE), 0)
        == lax.broadcasted_iota(jnp.int32, (window, 2 * LANE), 1) + shift,
        1.0,
        0.0,
    ).astype(BF)

    def cut(k, start):
        for g in range(RING):
            part = buf[g, :, :, :, pl.ds(pl.multiple_of(start + low, LANE), window)]
            cuts[k, pl.ds(g * line, line), :] = dot(part.reshape(line, window), move).astype(BF)

    strip = 32

    def silu_step(i, carry):
        r = pl.ds(pl.multiple_of(i * strip, strip), strip)
        gate_proj, up_proj = gate_acc[r, :], up_acc[r, :]
        sig = jax.nn.sigmoid(gate_proj)
        activated = gate_proj * sig
        acts[r, pl.ds(2 * ff, ff)] = (activated * up_proj).astype(BF)
        gate_acc[r, :] = up_proj * sig * (1.0 + gate_proj * (1.0 - sig))
        up_acc[r, :] = activated
        return carry

    def finish(i, carry):
        r = pl.ds(pl.multiple_of(i * strip, strip), strip)
        down_proj = down_acc[r, :]
        hidden_grad = gate_rows[r, 0:1] * down_proj
        acts[r, pl.ds(0, ff)] = (hidden_grad * gate_acc[r, :]).astype(BF)
        acts[r, pl.ds(ff, ff)] = (hidden_grad * up_acc[r, :]).astype(BF)
        hidden = acts[r, pl.ds(2 * ff, ff)].astype(F32)
        total = jnp.sum(hidden * down_proj, axis=1, keepdims=True)
        high = total.astype(BF)
        low_part = (total - high.astype(F32)).astype(BF)
        lanes = lax.broadcasted_iota(jnp.int32, (strip, LANE), 1)
        score[r, :] = jnp.where(
            lanes < LANE // 2, high.astype(F32), low_part.astype(F32)
        ).astype(BF)
        return carry

    steps, plain = width // chunk, straight // chunk
    strips = cap * slots // strip
    lax.fori_loop(0, plain, x_step, 0)
    p2.four()
    p3.four()
    xa[3].three()
    xb[0].three()
    xb[3].two()
    for ring in xa:
        ring.four()
    lax.fori_loop(plain, steps, x_step, 0)
    xb[1].three()
    xb[2].three()
    cut(0, x0)
    lax.fori_loop(0, strips, silu_step, 0)
    p2.five()
    p3.five()
    xb[3].three()
    p2.six()
    p3.six()
    lax.fori_loop(0, plain, dy_step, 0)
    for ring in xb:
        ring.four()
    lax.fori_loop(plain, steps, dy_step, 0)
    cut(1, dy0)
    lax.fori_loop(0, strips, finish, 0)
    links.drain()


def return_kernel(
    dims,
    acts, score, meta_all, cuts, w_gate, w_up,
    slot_grads, input_grads, gate_grads,
    held_all, wg, wu, far, up_buf, down_buf, far_in, sum_in, score_in,
    row_at, gate_at, rows_buf, turned, by_token, block_sum,
    y_far, y_sums, y_total, z_far, z_sums, z_total, stage,
    send, recv, local, out_sem,
):
    per, width, cap, top, ff = dims
    slots = RING * RING * CORES
    rows = cap * slots
    part = width // RING
    half = part // 2
    links = Links(send, recv)
    y, z, c, t = links.y, links.z, links.c, links.t
    a = acts
    me = lax.axis_index("expert")
    own = pltpu.make_async_copy(acts, held_all.at[y, z, c], local.at[0])
    weights = [
        pltpu.make_async_copy(w_gate, wg, local.at[2]),
        pltpu.make_async_copy(w_up, wu, local.at[3]),
    ]
    for copy in [own] + weights:
        copy.start()
    own.wait()
    right, left, across = links.to(t=up1(t)), links.to(t=down1(t)), links.to(t=up1(up1(t)))
    links.greet(links.plane() + [right, left, across])

    def piece(start, stop, y_first):
        middle = (start + stop) // 2
        spans = {None: (start, stop), 0: (start, middle), 1: (middle, stop)}

        def at(yy, zz, which):
            low, high = spans[which]
            return held_all.at[yy, zz, c, pl.ds(low, high - low), :]

        return Gather(links, at, y_first)

    group_rows = rows // RING
    line_tokens = per * slots // RING
    width_own = width // slots

    def place_rows():
        ids = lax.broadcasted_iota(jnp.int32, (slots, 1), 0)
        for g in range(RING):
            row, gate, _ = entries(
                meta_all[pl.ds(g * line_tokens, line_tokens), :], ids, per, cap, top
            )
            row_at[g] = row
            gate_at[g] = gate

    several = 4

    def turn_step(i, carry):
        for g in range(RING):
            toks = pl.ds(g * line_tokens, line_tokens)
            chosen, weighed = [], []
            for j in range(several):
                slot = i * several + j
                pick = picks(row_at[g, pl.ds(slot, 1), :], group_rows)
                chosen.append(pick.astype(BF))
                weighed.append((pick * gate_at[g, pl.ds(slot, 1), :]).astype(BF))
            for k, lhs in enumerate((chosen, weighed)):
                found = dot(jnp.concatenate(lhs, axis=0), cuts[k, toks, :])
                for j in range(several):
                    rows_buf[j, k, pl.ds(g * group_rows, group_rows), :] = found[
                        j * group_rows : (j + 1) * group_rows
                    ].astype(BF)
        for j in range(several):
            for k in range(2):
                turned[i * several + j, k] = jnp.transpose(rows_buf[j, k])[:width_own]
        return carry

    g0 = piece(0, rows // 2, True)
    g1 = piece(rows // 2, rows, False)
    g0.one()
    g1.one()
    for copy in weights:
        copy.wait()

    def fill(out, quarter, low, count, extra=None):
        r = pl.ds(pl.multiple_of(quarter * part + low, LANE), count)
        sums = dot(a[:, 0:ff], wg[r, :], NT) + dot(a[:, ff : 2 * ff], wu[r, :], NT)
        for more in extra or ():
            sums = sums + more[...].astype(F32)
        out[:, pl.ds(low, count)] = sums.astype(BF)

    pieces = []
    for low in (0, half):
        first = half // (2 * LANE) * LANE + LANE
        pieces.append(((low, first), (low + first, half - first)))

    def cols_of(span):
        return pl.ds(*span)

    far_copies, straight, summed = [], [], []

    def send_far(h):
        one, two = pieces[h]
        fill(far, up1(up1(t)), h * half, half)
        far_copies.append(
            (
                links.start(far.at[:, cols_of(one)], far_in.at[:, cols_of(one)], right),
                links.start(far.at[:, cols_of(two)], far_in.at[:, cols_of(two)], left),
            )
        )

    def send_straight(h):
        one, two = pieces[h]
        fill(up_buf, up1(t), *two)
        d_right = links.start(
            up_buf.at[:, cols_of(two)], sum_in.at[0, :, cols_of(two)], right
        )
        fill(down_buf, down1(t), *one)
        d_left = links.start(
            down_buf.at[:, cols_of(one)], sum_in.at[1, :, cols_of(one)], left
        )
        straight.append((d_right, d_left))

    def send_summed(h):
        one, two = pieces[h]
        f_right, f_left = far_copies[h]
        f_right.wait_recv()
        fill(up_buf, up1(t), *one, [far_in.at[:, cols_of(one)]])
        s_right = links.start(
            up_buf.at[:, cols_of(one)], sum_in.at[0, :, cols_of(one)], right
        )
        f_left.wait_recv()
        fill(down_buf, down1(t), *two, [far_in.at[:, cols_of(two)]])
        s_left = links.start(
            down_buf.at[:, cols_of(two)], sum_in.at[1, :, cols_of(two)], left
        )
        summed.append((s_right, s_left))

    wide = part + LANE
    shared, chosen_rows = [], []

    def to_tokens(h, score_rows=None):
        for copy in (*straight[h], *summed[h]):
            copy.wait_recv()
        cols = pl.ds(h * half, half)
        fill(far_in, t, h * half, half, [sum_in.at[0, :, cols], sum_in.at[1, :, cols]])
        low, stop = h * half, half if h == 0 else wide
        for g in range(RING):
            chosen = picks(row_at[g, pl.ds(me, 1), :], group_rows).astype(BF)
            r = pl.ds(g * group_rows, group_rows)
            found = dot(chosen, far_in[r, cols], TN).astype(BF)
            by_token[g, :, :, :, cols] = found.reshape(RING, CORES, per, half)
            if h == 1:
                named = meta_all[pl.ds(g * line_tokens, line_tokens), :].astype(F32)
                lanes = lax.broadcasted_iota(jnp.int32, (line_tokens, LANE), 1)
                found = dot(
                    chosen, score_rows[g * group_rows : (g + 1) * group_rows], TN
                )
                found = jnp.where((named == me.astype(F32)) & (lanes < top), found, 0.0)
                by_token[g, :, :, :, pl.ds(part, LANE)] = found.astype(BF).reshape(
                    RING, CORES, per, LANE
                )
        cols = pl.ds(low, stop - low)
        shared.append(
            links.start(
                by_token.at[:, :, 1 - c, :, cols], block_sum.at[:, :, :, cols], links.to(c=1 - c)
            )
        )

    def add_core(h):
        shared[h].wait_recv()
        low, stop = h * half, half if h == 0 else wide
        cols = pl.ds(low, stop - low)
        for g in range(RING):
            mine = by_token[g, :, pl.ds(c, 1), :, cols].reshape(RING, per, stop - low)
            block_sum[g, :, :, cols] = (
                block_sum[g, :, :, cols].astype(F32) + mine.astype(F32)
            ).astype(BF)

    rest = (wide - half) // 2
    spans = (
        (0, pieces[0][0][1], pieces[0][1][1]),
        (half, rest // 2, rest // 2),
        (half + rest, rest // 2, rest // 2),
    )
    firsts, seconds = [], []

    def ring_one(k):
        y_first = k < 2

        def at(v, lo, count):
            if y_first:
                return block_sum.at[v, :, :, pl.ds(lo, count)]
            return block_sum.at[:, v, :, pl.ds(lo, count)]

        firsts.append(
            RingSum(
                links,
                "y" if y_first else "z",
                at,
                lambda side, count: y_far.at[k, side, :, :, pl.ds(0, count)],
                lambda side, lo, count: y_sums.at[k, side, :, :, pl.ds(lo, count)],
                *spans[k],
            )
        )
        firsts[k].one()

    def ring_two(k):
        def put(lo, value):
            y_total[k, :, :, pl.ds(lo, value.shape[-1])] = value

        firsts[k].three(put)
        seconds.append(
            RingSum(
                links,
                "z" if k < 2 else "y",
                lambda v, lo, count: y_total.at[k, v, :, pl.ds(lo, count)],
                lambda side, count: z_far.at[k, side, :, pl.ds(0, count)],
                lambda side, lo, count: z_sums.at[k, side, :, pl.ds(lo, count)],
                0,
                *spans[k][1:],
            )
        )
        seconds[k].one()

    def ring_end(k):
        def put(lo, value):
            z_total[:, pl.ds(spans[k][0] + lo, value.shape[-1])] = value

        seconds[k].three(put)

    send_far(0)
    send_far(1)
    g0.two()
    g1.two()
    send_straight(0)
    place_rows()
    g0.three()
    g1.three()
    send_summed(0)
    send_straight(1)
    scores = [
        links.start(score, score_in.at[0], right),
        links.start(score, score_in.at[1], left),
        links.start(score, score_in.at[2], across),
    ]
    lax.fori_loop(0, slots // several // 2, turn_step, 0)
    send_summed(1)
    lax.fori_loop(slots // several // 2, slots // several, turn_step, 0)
    g0.four()
    g1.four()
    to_tokens(0)
    add_core(0)
    ring_one(0)
    for copy in scores:
        copy.wait_recv()
    total = jnp.zeros((rows, 1), F32)
    for ref in (score, score_in.at[0], score_in.at[1], score_in.at[2]):
        both = ref[...].astype(F32)
        total = total + (both[:, 0:1] + both[:, LANE // 2 : LANE // 2 + 1])
    score_rows = jnp.broadcast_to(total, (rows, LANE)).astype(BF)
    g0.five()
    g1.five()
    firsts[0].two()
    to_tokens(1, score_rows)
    ring_two(0)
    for gather in (g0, g1):
        gather.six()

    stored = []

    def grads(i):
        slot = i % 2
        if i >= 2:
            stored[i - 2].wait()

        def step(j, carry):
            place = (i // 2, (i % 2) * 2 + lax.div(j, CORES), lax.rem(j, CORES))
            own_slot = i * several + j
            both = dot(turned[own_slot, 0], held_all[(*place, slice(None), pl.ds(0, 2 * ff))])
            stage[slot, j, 0] = both[:, :ff].astype(BF)
            stage[slot, j, 1] = both[:, ff:].astype(BF)
            stage[slot, j, 2] = dot(
                turned[own_slot, 1], held_all[(*place, slice(None), pl.ds(2 * ff, ff))]
            ).astype(BF)
            return carry

        lax.fori_loop(0, several, step, 0)
        stored.append(
            pltpu.make_async_copy(
                stage.at[slot],
                slot_grads.at[pl.ds(i * several, several)],
                out_sem.at[i],
            )
        )
        stored[-1].start()

    add_core(1)
    ring_one(1)
    ring_one(2)
    seconds[0].two()
    grads(0)
    firsts[1].two()
    firsts[2].two()
    grads(1)
    grads(2)
    ring_two(1)
    ring_two(2)
    grads(3)
    seconds[1].two()
    seconds[2].two()
    grads(4)
    grads(5)
    for k in range(3):
        ring_end(k)
    input_grads[...] = z_total[:, pl.ds(0, part)]
    gate_grads[...] = z_total[:, pl.ds(part, LANE)]
    grads(6)
    grads(7)
    links.drain()
    stored[-2].wait()
    stored[-1].wait()


def combine_kernel(replicas, owners, slot_grads, out, copies, held, sems):
    experts = out.shape[0]
    load = pltpu.make_async_copy(
        slot_grads.at[pl.ds(experts, replicas)], copies, sems.at[2 * experts]
    )
    load.start()
    loads, stores = [], []
    for e in range(experts):
        loads.append(pltpu.make_async_copy(slot_grads.at[e], held.at[e], sems.at[e]))
        stores.append(pltpu.make_async_copy(held.at[e], out.at[e], sems.at[experts + e]))
        loads[e].start()
    load.wait()
    for e in range(experts):
        loads[e].wait()
        owned = owners[0] == e
        for r in range(1, replicas):
            owned = owned | (owners[r] == e)

        @pl.when(owned)
        def _():
            for k in range(3):
                total = held[e, k].astype(F32)
                for r in range(replicas):
                    same = jnp.where(owners[r] == e, 1.0, 0.0)
                    total = total + same * copies[r, k].astype(F32)
                held[e, k] = total.astype(BF)

        stores[e].start()
    for store in stores:
        store.wait()


def per_device(tokens, cotangent, gate_weights, route_slots, replica_owner, w_gate, w_up, w_down):
    slots = lax.axis_size("expert")
    per, width = tokens.shape
    top = route_slots.shape[1]
    cap = per * top * 3 // 2 // slots
    ff = w_gate.shape[2]
    rows = cap * slots
    part = width // RING
    padded = 16
    replicas = replica_owner.shape[0]
    experts = slots - replicas
    dims = (per, width, cap, top, ff)
    meta = jnp.concatenate(
        [
            route_slots.astype(BF),
            gate_weights,
            jnp.full((per, LANE - 2 * top), -1, BF),
        ],
        axis=1,
    )
    w_gate, w_up, w_down = w_gate[0], w_up[0], w_down[0]
    any_ = pl.BlockSpec(memory_space=pl.ANY)
    vmem = pl.BlockSpec(memory_space=pltpu.VMEM)
    line = per * slots // RING
    copies = 4 * GATHER_COPIES + 2 * (GATHER_COPIES - 4) + 8 * ACROSS_COPIES
    acts, score, cuts, meta_all = pl.pallas_call(
        functools.partial(dispatch_kernel, dims),
        name="dispatch",
        out_shape=(
            jax.ShapeDtypeStruct((rows, 3 * ff), BF),
            jax.ShapeDtypeStruct((rows, LANE), BF),
            jax.ShapeDtypeStruct((2, per * slots, 2 * LANE), BF),
            jax.ShapeDtypeStruct((per * slots, LANE), BF),
        ),
        in_specs=[any_] * 6,
        out_specs=(vmem,) * 4,
        scratch_shapes=[
            pltpu.VMEM((RING, RING, CORES, per, LANE + 2 * width), BF),
            pltpu.VMEM((width, ff), BF),
            pltpu.VMEM((width, ff), BF),
            pltpu.VMEM((width, ff), BF),
            pltpu.VMEM((rows, 512), BF),
            pltpu.VMEM((rows, ff), F32),
            pltpu.VMEM((rows, ff), F32),
            pltpu.VMEM((rows, ff), F32),
            pltpu.VMEM((RING, rows // RING, line), BF),
            pltpu.VMEM((rows, LANE), F32),
            pltpu.SemaphoreType.DMA((copies,)),
            pltpu.SemaphoreType.DMA((copies,)),
            pltpu.SemaphoreType.DMA((6,)),
        ],
        compiler_params=pltpu.CompilerParams(
            collective_id=0, has_side_effects=True, vmem_limit_bytes=56 * MIB
        ),
    )(tokens, cotangent, meta, w_gate, w_up, w_down)
    copies = 2 * GATHER_COPIES + 15 + 2 + 6 * RING_COPIES
    own = width // slots
    wide = part + LANE
    half = part // 2
    piece = half // (2 * LANE) * LANE + LANE
    slot_grads, input_grads, gate_grads = pl.pallas_call(
        functools.partial(return_kernel, dims),
        name="grads_back",
        out_shape=(
            jax.ShapeDtypeStruct((slots, 3, own, ff), BF),
            jax.ShapeDtypeStruct((per, part), BF),
            jax.ShapeDtypeStruct((per, LANE), BF),
        ),
        in_specs=[vmem, vmem, vmem, vmem, any_, any_],
        out_specs=(any_, vmem, vmem),
        scratch_shapes=[
            pltpu.VMEM((RING, RING, CORES, rows, 3 * ff), BF),
            pltpu.VMEM((width, ff), BF),
            pltpu.VMEM((width, ff), BF),
            pltpu.VMEM((rows, part), BF),
            pltpu.VMEM((rows, part), BF),
            pltpu.VMEM((rows, part), BF),
            pltpu.VMEM((rows, part), BF),
            pltpu.VMEM((2, rows, part), BF),
            pltpu.VMEM((3, rows, LANE), BF),
            pltpu.VMEM((RING, slots, line), F32),
            pltpu.VMEM((RING, slots, line), F32),
            pltpu.VMEM((4, 2, rows, 2 * LANE), BF),
            pltpu.VMEM((slots, 2, own, rows), BF),
            pltpu.VMEM((RING, RING, CORES, per, wide), BF),
            pltpu.VMEM((RING, RING, per, wide), BF),
            pltpu.VMEM((3, 2, RING, per, piece), BF),
            pltpu.VMEM((3, 2, RING, per, half), BF),
            pltpu.VMEM((3, RING, per, half), BF),
            pltpu.VMEM((3, 2, per, piece), BF),
            pltpu.VMEM((3, 2, per, half), BF),
            pltpu.VMEM((per, wide), BF),
            pltpu.VMEM((2, 4, 3, own, ff), BF),
            pltpu.SemaphoreType.DMA((copies,)),
            pltpu.SemaphoreType.DMA((copies,)),
            pltpu.SemaphoreType.DMA((4,)),
            pltpu.SemaphoreType.DMA((slots // 4,)),
        ],
        compiler_params=pltpu.CompilerParams(
            collective_id=1, has_side_effects=True, vmem_limit_bytes=62 * MIB
        ),
    )(acts, score, meta_all, cuts, w_gate, w_up)
    expert_grads = pl.pallas_call(
        functools.partial(combine_kernel, replicas),
        name="combine",
        out_shape=jax.ShapeDtypeStruct((experts, 3, own, ff), BF),
        in_specs=[pl.BlockSpec(memory_space=pltpu.SMEM), any_],
        out_specs=any_,
        scratch_shapes=[
            pltpu.VMEM((replicas, 3, own, ff), BF),
            pltpu.VMEM((experts, 3, own, ff), BF),
            pltpu.SemaphoreType.DMA((2 * experts + 1,)),
        ],
        compiler_params=pltpu.CompilerParams(vmem_limit_bytes=60 * MIB),
    )(replica_owner, slot_grads)
    return input_grads, gate_grads[:, :top], jnp.transpose(expert_grads, (0, 2, 1, 3))


def solution(mesh):
    in_specs = (
        P("expert", None),
        P("expert", None),
        P("expert", None),
        P("expert", None),
        P(),
        P("expert", None, "tensor"),
        P("expert", None, "tensor"),
        P("expert", None, "tensor"),
    )
    out_specs = (P("expert", "tensor"), P("expert", None), P(None, "expert", None, "tensor"))
    return jax.shard_map(
        per_device, mesh=mesh, in_specs=in_specs, out_specs=out_specs, check_vma=False
    )
```

```python
import functools

import jax
import jax.numpy as jnp
from jax import lax
from jax.experimental import pallas as pl
from jax.experimental.pallas import tpu as pltpu
from jax.sharding import PartitionSpec as P

MESH = pl.DeviceIdType.MESH
BF = jnp.bfloat16
F32 = jnp.float32
LANE = 128
SHARED = 6
CHUNK = 1024
RING = 4
CORES = 2
MIB = 1 << 20
NT = (((1,), (1,)), ((), ()))
TN = (((0,), (0,)), ((), ()))


def dot(a, b, dims=None):
    if dims is None:
        return jnp.dot(a, b, preferred_element_type=F32)
    return lax.dot_general(a, b, dims, preferred_element_type=F32)


def up1(v):
    return lax.rem(v + 1, RING)


def down1(v):
    return lax.rem(v + RING - 1, RING)


def position():
    e = lax.axis_index("expert")
    t = lax.axis_index("tensor")
    return lax.div(e, CORES * RING), lax.rem(lax.div(e, CORES), RING), lax.rem(e, CORES), t


class Links:
    def __init__(self, send, recv):
        self.send, self.recv, self.count, self.started = send, recv, 0, []
        self.y, self.z, self.c, self.t = position()

    def to(self, y=None, z=None, c=None, t=None):
        y = self.y if y is None else y
        z = self.z if z is None else z
        c = self.c if c is None else c
        t = self.t if t is None else t
        return ((y * RING + z) * CORES + c, t)

    def start(self, src, dst, device):
        copy = pltpu.make_async_remote_copy(
            src_ref=src,
            dst_ref=dst,
            send_sem=self.send.at[self.count],
            recv_sem=self.recv.at[self.count],
            device_id=device,
            device_id_type=MESH,
        )
        self.count += 1
        copy.start()
        self.started.append(copy)
        return copy

    def greet(self, devices):
        barrier = pltpu.get_barrier_semaphore()
        for device in devices:
            pl.semaphore_signal(barrier, inc=1, device_id=device, device_id_type=MESH)
        pl.semaphore_wait(barrier, len(devices))

    def plane(self):
        return [
            self.to(y=up1(self.y)),
            self.to(y=down1(self.y)),
            self.to(z=up1(self.z)),
            self.to(z=down1(self.z)),
            self.to(c=1 - self.c),
        ]

    def drain(self):
        for copy in self.started:
            copy.wait_send()


class Gather:
    def __init__(self, links, at, y_first, handed=True):
        self.l, self.at, self.y_first, self.handed = links, at, y_first, handed
        self.first = links.y if y_first else links.z
        self.second = links.z if y_first else links.y

    def place(self, first, second, part=None):
        return self.at(first, second, part) if self.y_first else self.at(second, first, part)

    def along_first(self, v):
        return self.l.to(y=v) if self.y_first else self.l.to(z=v)

    def along_second(self, v):
        return self.l.to(z=v) if self.y_first else self.l.to(y=v)

    def copy(self, ref, device):
        return self.l.start(ref, ref, device)

    def hand_over(self, second):
        if self.handed:
            ref = self.place(slice(None), second)
            self.s.append(self.copy(ref, self.l.to(c=1 - self.l.c)))

    def lines(self):
        low, high = down1(self.second), up1(self.second)
        return [self.second, low, high, up1(high)]

    def one(self):
        own = self.place(self.first, self.second)
        self.m1 = self.copy(own, self.along_first(up1(self.first)))
        self.m2 = self.copy(own, self.along_first(down1(self.first)))

    def two(self):
        self.m1.wait_recv()
        self.m3 = self.copy(
            self.place(down1(self.first), self.second, 0), self.along_first(up1(self.first))
        )
        self.m2.wait_recv()
        self.m4 = self.copy(
            self.place(up1(self.first), self.second, 1), self.along_first(down1(self.first))
        )

    def three(self):
        self.m3.wait_recv()
        self.m4.wait_recv()
        line = self.place(slice(None), self.second)
        self.m5 = self.copy(line, self.along_second(up1(self.second)))
        self.m6 = self.copy(line, self.along_second(down1(self.second)))
        self.s = []
        self.hand_over(self.second)

    def four(self):
        low, high = down1(self.second), up1(self.second)
        self.m5.wait_recv()
        self.m7 = self.copy(self.place(slice(None), low, 0), self.along_second(high))
        self.hand_over(low)
        self.m6.wait_recv()
        self.m8 = self.copy(self.place(slice(None), high, 1), self.along_second(low))
        self.hand_over(high)

    def five(self):
        self.m7.wait_recv()
        self.m8.wait_recv()
        self.hand_over(up1(up1(self.second)))

    def six(self):
        for copy in self.s:
            copy.wait_recv()


GATHER_COPIES = 12


class Across:
    def __init__(self, links, at, whole):
        self.l, self.at, self.whole = links, at, whole

    def copy(self, ref, device):
        return self.l.start(ref, ref, device)

    def one(self):
        t = self.l.t
        self.m1 = self.copy(self.at(t), self.l.to(t=up1(t)))
        self.m2 = self.copy(self.at(t), self.l.to(t=down1(t)))

    def two(self):
        t = self.l.t
        self.m1.wait_recv()
        self.m3 = self.copy(self.at(down1(t), 0), self.l.to(t=up1(t)))
        self.m2.wait_recv()
        self.m4 = self.copy(self.at(up1(t), 1), self.l.to(t=down1(t)))

    def three(self):
        self.m3.wait_recv()
        self.m4.wait_recv()
        self.s = self.copy(self.whole, self.l.to(c=1 - self.l.c))

    def four(self):
        self.s.wait_recv()


ACROSS_COPIES = 5


class RingSum:
    def __init__(self, links, axis, at, far, sums, low, first, second):
        self.l, self.axis, self.at, self.far, self.sums = links, axis, at, far, sums
        self.me = getattr(links, axis)
        self.high, self.down = up1(self.me), down1(self.me)
        self.low, self.first, self.second = low, first, second

    def to(self, v):
        return self.l.to(**{self.axis: v})

    def part(self, v, k):
        if k == 0:
            return self.at(v, self.low, self.first)
        return self.at(v, self.low + self.first, self.second)

    def sum_part(self, side, k):
        low, count = (0, self.first) if k == 0 else (self.first, self.second)
        return self.sums(side, low, count)

    def one(self):
        across, start = up1(self.high), self.l.start
        high, down = self.to(self.high), self.to(self.down)
        self.f0 = start(self.part(across, 0), self.far(0, self.first), high)
        self.f1 = start(self.part(across, 1), self.far(1, self.second), down)
        self.d0 = start(self.part(self.high, 1), self.sum_part(0, 1), high)
        self.d1 = start(self.part(self.down, 0), self.sum_part(1, 0), down)

    def two(self):
        self.f0.wait_recv()
        ref = self.part(self.high, 0)
        ref[...] = (ref[...].astype(F32) + self.far(0, self.first)[...].astype(F32)).astype(BF)
        self.s0 = self.l.start(ref, self.sum_part(0, 0), self.to(self.high))
        self.f1.wait_recv()
        ref = self.part(self.down, 1)
        ref[...] = (ref[...].astype(F32) + self.far(1, self.second)[...].astype(F32)).astype(BF)
        self.s1 = self.l.start(ref, self.sum_part(1, 1), self.to(self.down))

    def three(self, put):
        for copy in (self.d0, self.d1, self.s0, self.s1):
            copy.wait_recv()
        for k in range(2):
            total = self.part(self.me, k)[...].astype(F32)
            for side in range(2):
                total = total + self.sum_part(side, k)[...].astype(F32)
            put(0 if k == 0 else self.first, total.astype(BF))


RING_COPIES = 6


def entries(meta, slot, per, cap, top):
    count = meta.shape[0]
    pick = (
        lax.broadcasted_iota(jnp.int32, (2 * top, LANE), 0)
        == lax.broadcasted_iota(jnp.int32, (2 * top, LANE), 1)
    ).astype(F32).astype(BF)
    turned = dot(pick, meta, NT)
    slot = slot.astype(F32)
    hit = jnp.zeros((slot.shape[0], count), F32)
    gate = jnp.zeros((slot.shape[0], count), F32)
    for k in range(top):
        same = turned[k : k + 1] == slot
        hit = hit + jnp.where(same, 1.0, 0.0)
        gate = gate + jnp.where(same, turned[top + k : top + k + 1], 0.0)
    earlier = lax.broadcasted_iota(jnp.int32, (count, count), 0)
    token = lax.broadcasted_iota(jnp.int32, (count, count), 1)
    before = jnp.where(
        (earlier < token) & (lax.div(earlier, per) == lax.div(token, per)), 1.0, 0.0
    ).astype(BF)
    place = dot(hit.astype(BF), before)
    block = lax.div(lax.broadcasted_iota(jnp.int32, hit.shape, 1), per).astype(F32)
    row = jnp.where(hit > 0.5, block * cap + place, -1.0)
    return row, gate, turned


def picks(row, group_rows):
    lines = lax.broadcasted_iota(jnp.int32, (group_rows, row.shape[1]), 0).astype(F32)
    return jnp.where(row == lines, 1.0, 0.0)


def dispatch_kernel(
    dims,
    tokens, cotangent, meta, w_gate, w_up, w_down,
    acts, score, cuts, meta_all,
    buf, wg, wu, wd, rows_buf, gate_acc, up_acc, down_acc, select, gate_rows,
    send, recv, local,
):
    per, width, cap, top, ff = dims
    slots = RING * RING * CORES
    group_rows = cap * slots // RING
    line = per * slots // RING
    links = Links(send, recv)
    y, z, c = links.y, links.z, links.c
    me = lax.axis_index("expert")
    x0, dy0 = LANE, LANE + width
    end = LANE + 2 * width
    loads = [
        pltpu.make_async_copy(meta, buf.at[y, z, c, :, pl.ds(0, LANE)], local.at[0]),
        pltpu.make_async_copy(tokens, buf.at[y, z, c, :, pl.ds(x0, width)], local.at[1]),
        pltpu.make_async_copy(cotangent, buf.at[y, z, c, :, pl.ds(dy0, width)], local.at[2]),
    ]
    weights = [
        pltpu.make_async_copy(w_gate, wg, local.at[3]),
        pltpu.make_async_copy(w_up, wu, local.at[4]),
        pltpu.make_async_copy(w_down, wd, local.at[5]),
    ]
    for copy in loads + weights:
        copy.start()
    for copy in loads:
        copy.wait()
    t = links.t
    links.greet(links.plane() + [links.to(t=up1(t)), links.to(t=down1(t))])

    def piece(start, size, y_first, handed=True):
        middle = size // (2 * LANE) * LANE
        spans = {None: (0, size), 0: (0, middle), 1: (middle, size - middle)}

        def at(yy, zz, part):
            low, count = spans[part]
            return buf.at[yy, zz, c, :, pl.ds(pl.multiple_of(start + low, LANE), count)]

        return Gather(links, at, y_first, handed)

    quarter = SHARED * LANE
    straight = width - RING * quarter

    def across(first, gather):
        def ring(line):
            def at(owner, part=None):
                low, count = {
                    None: (0, quarter),
                    0: (0, quarter // (2 * LANE) * LANE),
                    1: (quarter // (2 * LANE) * LANE, quarter - quarter // (2 * LANE) * LANE),
                }[part]
                cols = pl.ds(pl.multiple_of(first + owner * quarter + low, LANE), count)
                if gather.y_first:
                    return buf.at[:, line, c, :, cols]
                return buf.at[line, :, c, :, cols]

            cols = pl.ds(first, RING * quarter)
            if gather.y_first:
                whole = buf.at[:, line, c, :, cols]
            else:
                whole = buf.at[line, :, c, :, cols]
            return Across(links, at, whole)

        return [ring(line) for line in gather.lines()]

    qx0, qdy0 = x0 + straight, dy0 + straight
    qa = piece(qx0 + t * quarter, quarter, True, False)
    qb = piece(qdy0 + t * quarter, quarter, False, False)
    xa, xb = across(qx0, qa), across(qdy0, qb)
    half = straight // (2 * LANE) * LANE
    p0 = piece(0, x0 + half, True)
    p1 = piece(x0 + half, straight - half, False)
    p2 = piece(dy0, half, True)
    p3 = piece(dy0 + half, straight - half, False)
    qa.one()
    qb.one()
    qa.two()
    qb.two()
    p0.one()
    p1.one()
    qa.three()
    xa[0].one()
    qb.three()
    xb[0].one()
    p0.two()
    p1.two()
    qa.four()
    xa[1].one()
    xa[2].one()
    qb.four()
    p0.three()
    p1.three()
    qa.five()
    xa[3].one()
    qb.five()
    p2.one()
    p3.one()
    xa[0].two()
    xb[1].one()
    xb[2].one()
    p2.two()
    p3.two()
    xa[1].two()
    xa[2].two()
    xb[3].one()
    p0.four()
    p1.four()
    p2.three()
    p3.three()
    xa[3].two()
    xa[0].three()
    xb[0].two()
    p0.five()
    p1.five()
    xa[1].three()
    xa[2].three()
    xb[1].two()
    xb[2].two()
    p0.six()
    p1.six()

    for copy in weights:
        copy.wait()
    my_slot = jnp.full((8, 1), me, jnp.int32)
    for g in range(RING):
        part = buf[g, :, :, :, pl.ds(0, LANE)].reshape(line, LANE)
        meta_all[pl.ds(g * line, line), :] = part
        row, gate, _ = entries(part, my_slot, per, cap, top)
        chosen = picks(row[0:1], group_rows)
        select[g] = chosen.astype(BF)
        gate_rows[pl.ds(g * group_rows, group_rows), :] = jnp.broadcast_to(
            jnp.sum(chosen * gate[0:1], axis=1, keepdims=True), (group_rows, LANE)
        )

    chunk = CHUNK

    def fill_rows(start):
        for g in range(RING):
            part = buf[g, :, :, :, pl.ds(start, chunk)].reshape(line, chunk)
            rows_buf[pl.ds(g * group_rows, group_rows), :] = dot(select[g], part).astype(BF)

    gate_acc[...] = jnp.zeros_like(gate_acc)
    up_acc[...] = jnp.zeros_like(up_acc)
    down_acc[...] = jnp.zeros_like(down_acc)

    def x_step(i, carry):
        off = pl.multiple_of(i * chunk, chunk)
        fill_rows(pl.multiple_of(x0 + i * chunk, LANE))
        gate_acc[...] += dot(rows_buf[...], wg[pl.ds(off, chunk), :])
        up_acc[...] += dot(rows_buf[...], wu[pl.ds(off, chunk), :])
        return carry

    def dy_step(i, carry):
        off = pl.multiple_of(i * chunk, chunk)
        fill_rows(pl.multiple_of(dy0 + i * chunk, LANE))
        down_acc[...] += dot(rows_buf[...], wd[pl.ds(off, chunk), :])
        return carry

    own = width // slots
    window = 3 * LANE
    low = jnp.minimum(lax.div(me * own, LANE) * LANE, width - window)
    shift = me * own - low
    move = jnp.where(
        lax.broadcasted_iota(jnp.int32, (window, 2 * LANE), 0)
        == lax.broadcasted_iota(jnp.int32, (window, 2 * LANE), 1) + shift,
        1.0,
        0.0,
    ).astype(BF)

    def cut(k, start):
        for g in range(RING):
            part = buf[g, :, :, :, pl.ds(pl.multiple_of(start + low, LANE), window)]
            cuts[k, pl.ds(g * line, line), :] = dot(part.reshape(line, window), move).astype(BF)

    strip = 32

    def silu_step(i, carry):
        r = pl.ds(pl.multiple_of(i * strip, strip), strip)
        gate_proj, up_proj = gate_acc[r, :], up_acc[r, :]
        sig = jax.nn.sigmoid(gate_proj)
        activated = gate_proj * sig
        acts[r, pl.ds(2 * ff, ff)] = (activated * up_proj).astype(BF)
        gate_acc[r, :] = up_proj * sig * (1.0 + gate_proj * (1.0 - sig))
        up_acc[r, :] = activated
        return carry

    def finish(i, carry):
        r = pl.ds(pl.multiple_of(i * strip, strip), strip)
        down_proj = down_acc[r, :]
        hidden_grad = gate_rows[r, 0:1] * down_proj
        acts[r, pl.ds(0, ff)] = (hidden_grad * gate_acc[r, :]).astype(BF)
        acts[r, pl.ds(ff, ff)] = (hidden_grad * up_acc[r, :]).astype(BF)
        hidden = acts[r, pl.ds(2 * ff, ff)].astype(F32)
        total = jnp.sum(hidden * down_proj, axis=1, keepdims=True)
        high = total.astype(BF)
        low_part = (total - high.astype(F32)).astype(BF)
        lanes = lax.broadcasted_iota(jnp.int32, (strip, LANE), 1)
        score[r, :] = jnp.where(
            lanes < LANE // 2, high.astype(F32), low_part.astype(F32)
        ).astype(BF)
        return carry

    steps, plain = width // chunk, straight // chunk
    strips = cap * slots // strip
    lax.fori_loop(0, plain, x_step, 0)
    p2.four()
    p3.four()
    xa[3].three()
    xb[0].three()
    xb[3].two()
    for ring in xa:
        ring.four()
    lax.fori_loop(plain, steps, x_step, 0)
    xb[1].three()
    xb[2].three()
    cut(0, x0)
    lax.fori_loop(0, strips, silu_step, 0)
    p2.five()
    p3.five()
    xb[3].three()
    p2.six()
    p3.six()
    lax.fori_loop(0, plain, dy_step, 0)
    for ring in xb:
        ring.four()
    lax.fori_loop(plain, steps, dy_step, 0)
    cut(1, dy0)
    lax.fori_loop(0, strips, finish, 0)
    links.drain()


def return_kernel(
    dims,
    acts, score, meta_all, cuts, w_gate, w_up,
    slot_grads, input_grads, gate_grads,
    held_all, wg, wu, far, up_buf, down_buf, far_in, sum_in, score_in,
    row_at, gate_at, rows_buf, turned, by_token, block_sum,
    y_far, y_sums, y_total, z_far, z_sums, z_total, stage,
    send, recv, local, out_sem,
):
    per, width, cap, top, ff = dims
    slots = RING * RING * CORES
    rows = cap * slots
    part = width // RING
    half = part // 2
    links = Links(send, recv)
    y, z, c, t = links.y, links.z, links.c, links.t
    a = acts
    me = lax.axis_index("expert")
    own = pltpu.make_async_copy(acts, held_all.at[y, z, c], local.at[0])
    weights = [
        pltpu.make_async_copy(w_gate, wg, local.at[2]),
        pltpu.make_async_copy(w_up, wu, local.at[3]),
    ]
    for copy in [own] + weights:
        copy.start()
    own.wait()
    right, left, across = links.to(t=up1(t)), links.to(t=down1(t)), links.to(t=up1(up1(t)))
    links.greet(links.plane() + [right, left, across])

    def piece(start, stop, y_first):
        middle = (start + stop) // 2
        spans = {None: (start, stop), 0: (start, middle), 1: (middle, stop)}

        def at(yy, zz, which):
            low, high = spans[which]
            return held_all.at[yy, zz, c, pl.ds(low, high - low), :]

        return Gather(links, at, y_first)

    group_rows = rows // RING
    line_tokens = per * slots // RING
    width_own = width // slots

    def place_rows():
        ids = lax.broadcasted_iota(jnp.int32, (slots, 1), 0)
        for g in range(RING):
            row, gate, _ = entries(
                meta_all[pl.ds(g * line_tokens, line_tokens), :], ids, per, cap, top
            )
            row_at[g] = row
            gate_at[g] = gate

    several = 4

    def turn_step(i, carry):
        for g in range(RING):
            toks = pl.ds(g * line_tokens, line_tokens)
            chosen, weighed = [], []
            for j in range(several):
                slot = i * several + j
                pick = picks(row_at[g, pl.ds(slot, 1), :], group_rows)
                chosen.append(pick.astype(BF))
                weighed.append((pick * gate_at[g, pl.ds(slot, 1), :]).astype(BF))
            for k, lhs in enumerate((chosen, weighed)):
                found = dot(jnp.concatenate(lhs, axis=0), cuts[k, toks, :])
                for j in range(several):
                    rows_buf[j, k, pl.ds(g * group_rows, group_rows), :] = found[
                        j * group_rows : (j + 1) * group_rows
                    ].astype(BF)
        for j in range(several):
            for k in range(2):
                turned[i * several + j, k] = jnp.transpose(rows_buf[j, k])[:width_own]
        return carry

    g0 = piece(0, rows // 2, True)
    g1 = piece(rows // 2, rows, False)
    g0.one()
    g1.one()
    for copy in weights:
        copy.wait()

    def fill(out, quarter, low, count, extra=None):
        r = pl.ds(pl.multiple_of(quarter * part + low, LANE), count)
        sums = dot(a[:, 0:ff], wg[r, :], NT) + dot(a[:, ff : 2 * ff], wu[r, :], NT)
        for more in extra or ():
            sums = sums + more[...].astype(F32)
        out[:, pl.ds(low, count)] = sums.astype(BF)

    pieces = []
    for low in (0, half):
        first = half // (2 * LANE) * LANE + LANE
        pieces.append(((low, first), (low + first, half - first)))

    def cols_of(span):
        return pl.ds(*span)

    far_copies, straight, summed = [], [], []

    def send_far(h):
        one, two = pieces[h]
        fill(far, up1(up1(t)), h * half, half)
        far_copies.append(
            (
                links.start(far.at[:, cols_of(one)], far_in.at[:, cols_of(one)], right),
                links.start(far.at[:, cols_of(two)], far_in.at[:, cols_of(two)], left),
            )
        )

    def send_straight(h):
        one, two = pieces[h]
        fill(up_buf, up1(t), *two)
        d_right = links.start(
            up_buf.at[:, cols_of(two)], sum_in.at[0, :, cols_of(two)], right
        )
        fill(down_buf, down1(t), *one)
        d_left = links.start(
            down_buf.at[:, cols_of(one)], sum_in.at[1, :, cols_of(one)], left
        )
        straight.append((d_right, d_left))

    def send_summed(h):
        one, two = pieces[h]
        f_right, f_left = far_copies[h]
        f_right.wait_recv()
        fill(up_buf, up1(t), *one, [far_in.at[:, cols_of(one)]])
        s_right = links.start(
            up_buf.at[:, cols_of(one)], sum_in.at[0, :, cols_of(one)], right
        )
        f_left.wait_recv()
        fill(down_buf, down1(t), *two, [far_in.at[:, cols_of(two)]])
        s_left = links.start(
            down_buf.at[:, cols_of(two)], sum_in.at[1, :, cols_of(two)], left
        )
        summed.append((s_right, s_left))

    wide = part + LANE
    shared, chosen_rows = [], []

    def to_tokens(h, score_rows=None):
        for copy in (*straight[h], *summed[h]):
            copy.wait_recv()
        cols = pl.ds(h * half, half)
        fill(far_in, t, h * half, half, [sum_in.at[0, :, cols], sum_in.at[1, :, cols]])
        low, stop = h * half, half if h == 0 else wide
        for g in range(RING):
            chosen = picks(row_at[g, pl.ds(me, 1), :], group_rows).astype(BF)
            r = pl.ds(g * group_rows, group_rows)
            found = dot(chosen, far_in[r, cols], TN).astype(BF)
            by_token[g, :, :, :, cols] = found.reshape(RING, CORES, per, half)
            if h == 1:
                named = meta_all[pl.ds(g * line_tokens, line_tokens), :].astype(F32)
                lanes = lax.broadcasted_iota(jnp.int32, (line_tokens, LANE), 1)
                found = dot(
                    chosen, score_rows[g * group_rows : (g + 1) * group_rows], TN
                )
                found = jnp.where((named == me.astype(F32)) & (lanes < top), found, 0.0)
                by_token[g, :, :, :, pl.ds(part, LANE)] = found.astype(BF).reshape(
                    RING, CORES, per, LANE
                )
        cols = pl.ds(low, stop - low)
        shared.append(
            links.start(
                by_token.at[:, :, 1 - c, :, cols], block_sum.at[:, :, :, cols], links.to(c=1 - c)
            )
        )

    def add_core(h):
        shared[h].wait_recv()
        low, stop = h * half, half if h == 0 else wide
        cols = pl.ds(low, stop - low)
        for g in range(RING):
            mine = by_token[g, :, pl.ds(c, 1), :, cols].reshape(RING, per, stop - low)
            block_sum[g, :, :, cols] = (
                block_sum[g, :, :, cols].astype(F32) + mine.astype(F32)
            ).astype(BF)

    rest = (wide - half) // 2
    spans = (
        (0, pieces[0][0][1], pieces[0][1][1]),
        (half, rest // 2, rest // 2),
        (half + rest, rest // 2, rest // 2),
    )
    firsts, seconds = [], []

    def ring_one(k):
        y_first = k < 2

        def at(v, lo, count):
            if y_first:
                return block_sum.at[v, :, :, pl.ds(lo, count)]
            return block_sum.at[:, v, :, pl.ds(lo, count)]

        firsts.append(
            RingSum(
                links,
                "y" if y_first else "z",
                at,
                lambda side, count: y_far.at[k, side, :, :, pl.ds(0, count)],
                lambda side, lo, count: y_sums.at[k, side, :, :, pl.ds(lo, count)],
                *spans[k],
            )
        )
        firsts[k].one()

    def ring_two(k):
        def put(lo, value):
            y_total[k, :, :, pl.ds(lo, value.shape[-1])] = value

        firsts[k].three(put)
        seconds.append(
            RingSum(
                links,
                "z" if k < 2 else "y",
                lambda v, lo, count: y_total.at[k, v, :, pl.ds(lo, count)],
                lambda side, count: z_far.at[k, side, :, pl.ds(0, count)],
                lambda side, lo, count: z_sums.at[k, side, :, pl.ds(lo, count)],
                0,
                *spans[k][1:],
            )
        )
        seconds[k].one()

    def ring_end(k):
        def put(lo, value):
            z_total[:, pl.ds(spans[k][0] + lo, value.shape[-1])] = value

        seconds[k].three(put)

    send_far(0)
    send_far(1)
    g0.two()
    g1.two()
    send_straight(0)
    place_rows()
    g0.three()
    g1.three()
    send_summed(0)
    send_straight(1)
    scores = [
        links.start(score, score_in.at[0], right),
        links.start(score, score_in.at[1], left),
        links.start(score, score_in.at[2], across),
    ]
    lax.fori_loop(0, slots // several // 2, turn_step, 0)
    send_summed(1)
    lax.fori_loop(slots // several // 2, slots // several, turn_step, 0)
    g0.four()
    g1.four()
    to_tokens(0)
    add_core(0)
    ring_one(0)
    for copy in scores:
        copy.wait_recv()
    total = jnp.zeros((rows, 1), F32)
    for ref in (score, score_in.at[0], score_in.at[1], score_in.at[2]):
        both = ref[...].astype(F32)
        total = total + (both[:, 0:1] + both[:, LANE // 2 : LANE // 2 + 1])
    score_rows = jnp.broadcast_to(total, (rows, LANE)).astype(BF)
    g0.five()
    g1.five()
    firsts[0].two()
    to_tokens(1, score_rows)
    ring_two(0)
    for gather in (g0, g1):
        gather.six()

    stored = []

    def grads(i):
        slot = i % 2
        if i >= 2:
            stored[i - 2].wait()

        def step(j, carry):
            place = (i // 2, (i % 2) * 2 + lax.div(j, CORES), lax.rem(j, CORES))
            own_slot = i * several + j
            both = dot(turned[own_slot, 0], held_all[(*place, slice(None), pl.ds(0, 2 * ff))])
            stage[slot, j, 0] = both[:, :ff].astype(BF)
            stage[slot, j, 1] = both[:, ff:].astype(BF)
            stage[slot, j, 2] = dot(
                turned[own_slot, 1], held_all[(*place, slice(None), pl.ds(2 * ff, ff))]
            ).astype(BF)
            return carry

        lax.fori_loop(0, several, step, 0)
        stored.append(
            pltpu.make_async_copy(
                stage.at[slot],
                slot_grads.at[pl.ds(i * several, several)],
                out_sem.at[i],
            )
        )
        stored[-1].start()

    grads(0)
    add_core(1)
    ring_one(1)
    ring_one(2)
    seconds[0].two()
    grads(1)
    grads(2)
    firsts[1].two()
    firsts[2].two()
    grads(3)
    grads(4)
    ring_two(1)
    ring_two(2)
    grads(5)
    seconds[1].two()
    seconds[2].two()
    grads(6)
    for k in range(3):
        ring_end(k)
    input_grads[...] = z_total[:, pl.ds(0, part)]
    gate_grads[...] = z_total[:, pl.ds(part, LANE)]
    grads(7)
    links.drain()
    stored[-2].wait()
    stored[-1].wait()


def combine_kernel(replicas, owners, slot_grads, out, copies, held, sems):
    experts = out.shape[0]
    load = pltpu.make_async_copy(
        slot_grads.at[pl.ds(experts, replicas)], copies, sems.at[2 * experts]
    )
    load.start()
    loads, stores = [], []
    for e in range(experts):
        loads.append(pltpu.make_async_copy(slot_grads.at[e], held.at[e], sems.at[e]))
        stores.append(pltpu.make_async_copy(held.at[e], out.at[e], sems.at[experts + e]))
        loads[e].start()
    load.wait()
    for e in range(experts):
        loads[e].wait()
        owned = owners[0] == e
        for r in range(1, replicas):
            owned = owned | (owners[r] == e)

        @pl.when(owned)
        def _():
            for k in range(3):
                total = held[e, k].astype(F32)
                for r in range(replicas):
                    same = jnp.where(owners[r] == e, 1.0, 0.0)
                    total = total + same * copies[r, k].astype(F32)
                held[e, k] = total.astype(BF)

        stores[e].start()
    for store in stores:
        store.wait()


def per_device(tokens, cotangent, gate_weights, route_slots, replica_owner, w_gate, w_up, w_down):
    slots = lax.axis_size("expert")
    per, width = tokens.shape
    top = route_slots.shape[1]
    cap = per * top * 3 // 2 // slots
    ff = w_gate.shape[2]
    rows = cap * slots
    part = width // RING
    padded = 16
    replicas = replica_owner.shape[0]
    experts = slots - replicas
    dims = (per, width, cap, top, ff)
    meta = jnp.concatenate(
        [
            route_slots.astype(BF),
            gate_weights,
            jnp.full((per, LANE - 2 * top), -1, BF),
        ],
        axis=1,
    )
    w_gate, w_up, w_down = w_gate[0], w_up[0], w_down[0]
    any_ = pl.BlockSpec(memory_space=pl.ANY)
    vmem = pl.BlockSpec(memory_space=pltpu.VMEM)
    line = per * slots // RING
    copies = 4 * GATHER_COPIES + 2 * (GATHER_COPIES - 4) + 8 * ACROSS_COPIES
    acts, score, cuts, meta_all = pl.pallas_call(
        functools.partial(dispatch_kernel, dims),
        name="dispatch",
        out_shape=(
            jax.ShapeDtypeStruct((rows, 3 * ff), BF),
            jax.ShapeDtypeStruct((rows, LANE), BF),
            jax.ShapeDtypeStruct((2, per * slots, 2 * LANE), BF),
            jax.ShapeDtypeStruct((per * slots, LANE), BF),
        ),
        in_specs=[any_] * 6,
        out_specs=(vmem,) * 4,
        scratch_shapes=[
            pltpu.VMEM((RING, RING, CORES, per, LANE + 2 * width), BF),
            pltpu.VMEM((width, ff), BF),
            pltpu.VMEM((width, ff), BF),
            pltpu.VMEM((width, ff), BF),
            pltpu.VMEM((rows, CHUNK), BF),
            pltpu.VMEM((rows, ff), F32),
            pltpu.VMEM((rows, ff), F32),
            pltpu.VMEM((rows, ff), F32),
            pltpu.VMEM((RING, rows // RING, line), BF),
            pltpu.VMEM((rows, LANE), F32),
            pltpu.SemaphoreType.DMA((copies,)),
            pltpu.SemaphoreType.DMA((copies,)),
            pltpu.SemaphoreType.DMA((6,)),
        ],
        compiler_params=pltpu.CompilerParams(
            collective_id=0, has_side_effects=True, vmem_limit_bytes=56 * MIB
        ),
    )(tokens, cotangent, meta, w_gate, w_up, w_down)
    copies = 2 * GATHER_COPIES + 15 + 2 + 6 * RING_COPIES
    own = width // slots
    wide = part + LANE
    half = part // 2
    piece = half // (2 * LANE) * LANE + LANE
    slot_grads, input_grads, gate_grads = pl.pallas_call(
        functools.partial(return_kernel, dims),
        name="grads_back",
        out_shape=(
            jax.ShapeDtypeStruct((slots, 3, own, ff), BF),
            jax.ShapeDtypeStruct((per, part), BF),
            jax.ShapeDtypeStruct((per, LANE), BF),
        ),
        in_specs=[vmem, vmem, vmem, vmem, any_, any_],
        out_specs=(any_, vmem, vmem),
        scratch_shapes=[
            pltpu.VMEM((RING, RING, CORES, rows, 3 * ff), BF),
            pltpu.VMEM((width, ff), BF),
            pltpu.VMEM((width, ff), BF),
            pltpu.VMEM((rows, part), BF),
            pltpu.VMEM((rows, part), BF),
            pltpu.VMEM((rows, part), BF),
            pltpu.VMEM((rows, part), BF),
            pltpu.VMEM((2, rows, part), BF),
            pltpu.VMEM((3, rows, LANE), BF),
            pltpu.VMEM((RING, slots, line), F32),
            pltpu.VMEM((RING, slots, line), F32),
            pltpu.VMEM((4, 2, rows, 2 * LANE), BF),
            pltpu.VMEM((slots, 2, own, rows), BF),
            pltpu.VMEM((RING, RING, CORES, per, wide), BF),
            pltpu.VMEM((RING, RING, per, wide), BF),
            pltpu.VMEM((3, 2, RING, per, piece), BF),
            pltpu.VMEM((3, 2, RING, per, half), BF),
            pltpu.VMEM((3, RING, per, half), BF),
            pltpu.VMEM((3, 2, per, piece), BF),
            pltpu.VMEM((3, 2, per, half), BF),
            pltpu.VMEM((per, wide), BF),
            pltpu.VMEM((2, 4, 3, own, ff), BF),
            pltpu.SemaphoreType.DMA((copies,)),
            pltpu.SemaphoreType.DMA((copies,)),
            pltpu.SemaphoreType.DMA((4,)),
            pltpu.SemaphoreType.DMA((slots // 4,)),
        ],
        compiler_params=pltpu.CompilerParams(
            collective_id=1, has_side_effects=True, vmem_limit_bytes=62 * MIB
        ),
    )(acts, score, meta_all, cuts, w_gate, w_up)
    expert_grads = pl.pallas_call(
        functools.partial(combine_kernel, replicas),
        name="combine",
        out_shape=jax.ShapeDtypeStruct((experts, 3, own, ff), BF),
        in_specs=[pl.BlockSpec(memory_space=pltpu.SMEM), any_],
        out_specs=any_,
        scratch_shapes=[
            pltpu.VMEM((replicas, 3, own, ff), BF),
            pltpu.VMEM((experts, 3, own, ff), BF),
            pltpu.SemaphoreType.DMA((2 * experts + 1,)),
        ],
        compiler_params=pltpu.CompilerParams(vmem_limit_bytes=60 * MIB),
    )(replica_owner, slot_grads)
    return input_grads, gate_grads[:, :top], jnp.transpose(expert_grads, (0, 2, 1, 3))


def solution(mesh):
    in_specs = (
        P("expert", None),
        P("expert", None),
        P("expert", None),
        P("expert", None),
        P(),
        P("expert", None, "tensor"),
        P("expert", None, "tensor"),
        P("expert", None, "tensor"),
    )
    out_specs = (P("expert", "tensor"), P("expert", None), P(None, "expert", None, "tensor"))
    return jax.shard_map(
        per_device, mesh=mesh, in_specs=in_specs, out_specs=out_specs, check_vma=False
    )
```

```python
import functools

import jax
import jax.numpy as jnp
from jax import lax
from jax.experimental import pallas as pl
from jax.experimental.pallas import tpu as pltpu
from jax.sharding import PartitionSpec as P

MESH = pl.DeviceIdType.MESH
BF = jnp.bfloat16
F32 = jnp.float32
LANE = 128
SHARED = 6
CHUNK = 1024
RING = 4
CORES = 2
MIB = 1 << 20
NT = (((1,), (1,)), ((), ()))
TN = (((0,), (0,)), ((), ()))


def dot(a, b, dims=None):
    if dims is None:
        return jnp.dot(a, b, preferred_element_type=F32)
    return lax.dot_general(a, b, dims, preferred_element_type=F32)


def up1(v):
    return lax.rem(v + 1, RING)


def down1(v):
    return lax.rem(v + RING - 1, RING)


def position():
    e = lax.axis_index("expert")
    t = lax.axis_index("tensor")
    return lax.div(e, CORES * RING), lax.rem(lax.div(e, CORES), RING), lax.rem(e, CORES), t


class Links:
    def __init__(self, send, recv):
        self.send, self.recv, self.count, self.started = send, recv, 0, []
        self.y, self.z, self.c, self.t = position()

    def to(self, y=None, z=None, c=None, t=None):
        y = self.y if y is None else y
        z = self.z if z is None else z
        c = self.c if c is None else c
        t = self.t if t is None else t
        return ((y * RING + z) * CORES + c, t)

    def start(self, src, dst, device):
        copy = pltpu.make_async_remote_copy(
            src_ref=src,
            dst_ref=dst,
            send_sem=self.send.at[self.count],
            recv_sem=self.recv.at[self.count],
            device_id=device,
            device_id_type=MESH,
        )
        self.count += 1
        copy.start()
        self.started.append(copy)
        return copy

    def greet(self, devices):
        barrier = pltpu.get_barrier_semaphore()
        for device in devices:
            pl.semaphore_signal(barrier, inc=1, device_id=device, device_id_type=MESH)
        pl.semaphore_wait(barrier, len(devices))

    def plane(self):
        return [
            self.to(y=up1(self.y)),
            self.to(y=down1(self.y)),
            self.to(z=up1(self.z)),
            self.to(z=down1(self.z)),
            self.to(c=1 - self.c),
        ]

    def drain(self):
        for copy in self.started:
            copy.wait_send()


class Gather:
    def __init__(self, links, at, y_first, handed=True):
        self.l, self.at, self.y_first, self.handed = links, at, y_first, handed
        self.first = links.y if y_first else links.z
        self.second = links.z if y_first else links.y

    def place(self, first, second, part=None):
        return self.at(first, second, part) if self.y_first else self.at(second, first, part)

    def along_first(self, v):
        return self.l.to(y=v) if self.y_first else self.l.to(z=v)

    def along_second(self, v):
        return self.l.to(z=v) if self.y_first else self.l.to(y=v)

    def copy(self, ref, device):
        return self.l.start(ref, ref, device)

    def hand_over(self, second):
        if self.handed:
            ref = self.place(slice(None), second)
            self.s.append(self.copy(ref, self.l.to(c=1 - self.l.c)))

    def lines(self):
        low, high = down1(self.second), up1(self.second)
        return [self.second, low, high, up1(high)]

    def one(self):
        own = self.place(self.first, self.second)
        self.m1 = self.copy(own, self.along_first(up1(self.first)))
        self.m2 = self.copy(own, self.along_first(down1(self.first)))

    def two(self):
        self.m1.wait_recv()
        self.m3 = self.copy(
            self.place(down1(self.first), self.second, 0), self.along_first(up1(self.first))
        )
        self.m2.wait_recv()
        self.m4 = self.copy(
            self.place(up1(self.first), self.second, 1), self.along_first(down1(self.first))
        )

    def three(self):
        self.m3.wait_recv()
        self.m4.wait_recv()
        line = self.place(slice(None), self.second)
        self.m5 = self.copy(line, self.along_second(up1(self.second)))
        self.m6 = self.copy(line, self.along_second(down1(self.second)))
        self.s = []
        self.hand_over(self.second)

    def four(self):
        low, high = down1(self.second), up1(self.second)
        self.m5.wait_recv()
        self.m7 = self.copy(self.place(slice(None), low, 0), self.along_second(high))
        self.hand_over(low)
        self.m6.wait_recv()
        self.m8 = self.copy(self.place(slice(None), high, 1), self.along_second(low))
        self.hand_over(high)

    def five(self):
        self.m7.wait_recv()
        self.m8.wait_recv()
        self.hand_over(up1(up1(self.second)))

    def six(self):
        for copy in self.s:
            copy.wait_recv()


GATHER_COPIES = 12


class Across:
    def __init__(self, links, at, whole):
        self.l, self.at, self.whole = links, at, whole

    def copy(self, ref, device):
        return self.l.start(ref, ref, device)

    def one(self):
        t = self.l.t
        self.m1 = self.copy(self.at(t), self.l.to(t=up1(t)))
        self.m2 = self.copy(self.at(t), self.l.to(t=down1(t)))

    def two(self):
        t = self.l.t
        self.m1.wait_recv()
        self.m3 = self.copy(self.at(down1(t), 0), self.l.to(t=up1(t)))
        self.m2.wait_recv()
        self.m4 = self.copy(self.at(up1(t), 1), self.l.to(t=down1(t)))

    def three(self):
        self.m3.wait_recv()
        self.m4.wait_recv()
        self.s = self.copy(self.whole, self.l.to(c=1 - self.l.c))

    def four(self):
        self.s.wait_recv()


ACROSS_COPIES = 5


class RingSum:
    def __init__(self, links, axis, at, far, sums, low, first, second):
        self.l, self.axis, self.at, self.far, self.sums = links, axis, at, far, sums
        self.me = getattr(links, axis)
        self.high, self.down = up1(self.me), down1(self.me)
        self.low, self.first, self.second = low, first, second

    def to(self, v):
        return self.l.to(**{self.axis: v})

    def part(self, v, k):
        if k == 0:
            return self.at(v, self.low, self.first)
        return self.at(v, self.low + self.first, self.second)

    def sum_part(self, side, k):
        low, count = (0, self.first) if k == 0 else (self.first, self.second)
        return self.sums(side, low, count)

    def one(self):
        across, start = up1(self.high), self.l.start
        high, down = self.to(self.high), self.to(self.down)
        self.f0 = start(self.part(across, 0), self.far(0, self.first), high)
        self.f1 = start(self.part(across, 1), self.far(1, self.second), down)
        self.d0 = start(self.part(self.high, 1), self.sum_part(0, 1), high)
        self.d1 = start(self.part(self.down, 0), self.sum_part(1, 0), down)

    def two(self):
        self.f0.wait_recv()
        ref = self.part(self.high, 0)
        ref[...] = (ref[...].astype(F32) + self.far(0, self.first)[...].astype(F32)).astype(BF)
        self.s0 = self.l.start(ref, self.sum_part(0, 0), self.to(self.high))
        self.f1.wait_recv()
        ref = self.part(self.down, 1)
        ref[...] = (ref[...].astype(F32) + self.far(1, self.second)[...].astype(F32)).astype(BF)
        self.s1 = self.l.start(ref, self.sum_part(1, 1), self.to(self.down))

    def three(self, put):
        for copy in (self.d0, self.d1, self.s0, self.s1):
            copy.wait_recv()
        for k in range(2):
            total = self.part(self.me, k)[...].astype(F32)
            for side in range(2):
                total = total + self.sum_part(side, k)[...].astype(F32)
            put(0 if k == 0 else self.first, total.astype(BF))


RING_COPIES = 6


def entries(meta, slot, per, cap, top):
    count = meta.shape[0]
    pick = (
        lax.broadcasted_iota(jnp.int32, (2 * top, LANE), 0)
        == lax.broadcasted_iota(jnp.int32, (2 * top, LANE), 1)
    ).astype(F32).astype(BF)
    turned = dot(pick, meta, NT)
    slot = slot.astype(F32)
    hit = jnp.zeros((slot.shape[0], count), F32)
    gate = jnp.zeros((slot.shape[0], count), F32)
    for k in range(top):
        same = turned[k : k + 1] == slot
        hit = hit + jnp.where(same, 1.0, 0.0)
        gate = gate + jnp.where(same, turned[top + k : top + k + 1], 0.0)
    earlier = lax.broadcasted_iota(jnp.int32, (count, count), 0)
    token = lax.broadcasted_iota(jnp.int32, (count, count), 1)
    before = jnp.where(
        (earlier < token) & (lax.div(earlier, per) == lax.div(token, per)), 1.0, 0.0
    ).astype(BF)
    place = dot(hit.astype(BF), before)
    block = lax.div(lax.broadcasted_iota(jnp.int32, hit.shape, 1), per).astype(F32)
    row = jnp.where(hit > 0.5, block * cap + place, -1.0)
    return row, gate, turned


def picks(row, group_rows):
    lines = lax.broadcasted_iota(jnp.int32, (group_rows, row.shape[1]), 0).astype(F32)
    return jnp.where(row == lines, 1.0, 0.0)


def dispatch_kernel(
    dims,
    tokens, cotangent, meta, w_gate, w_up, w_down,
    acts, score, cuts, meta_all,
    buf, wg, wu, wd, rows_buf, gate_acc, up_acc, down_acc, select, gate_rows,
    send, recv, local,
):
    per, width, cap, top, ff = dims
    slots = RING * RING * CORES
    group_rows = cap * slots // RING
    line = per * slots // RING
    links = Links(send, recv)
    y, z, c = links.y, links.z, links.c
    me = lax.axis_index("expert")
    x0, dy0 = LANE, LANE + width
    end = LANE + 2 * width
    loads = [
        pltpu.make_async_copy(meta, buf.at[y, z, c, :, pl.ds(0, LANE)], local.at[0]),
        pltpu.make_async_copy(tokens, buf.at[y, z, c, :, pl.ds(x0, width)], local.at[1]),
        pltpu.make_async_copy(cotangent, buf.at[y, z, c, :, pl.ds(dy0, width)], local.at[2]),
    ]
    weights = [
        pltpu.make_async_copy(w_gate, wg, local.at[3]),
        pltpu.make_async_copy(w_up, wu, local.at[4]),
        pltpu.make_async_copy(w_down, wd, local.at[5]),
    ]
    for copy in loads + weights:
        copy.start()
    for copy in loads:
        copy.wait()
    t = links.t
    links.greet(links.plane() + [links.to(t=up1(t)), links.to(t=down1(t))])

    def piece(start, size, y_first, handed=True):
        middle = size // (2 * LANE) * LANE
        spans = {None: (0, size), 0: (0, middle), 1: (middle, size - middle)}

        def at(yy, zz, part):
            low, count = spans[part]
            return buf.at[yy, zz, c, :, pl.ds(pl.multiple_of(start + low, LANE), count)]

        return Gather(links, at, y_first, handed)

    quarter = SHARED * LANE
    straight = width - RING * quarter

    def across(first, gather):
        def ring(line):
            def at(owner, part=None):
                low, count = {
                    None: (0, quarter),
                    0: (0, quarter // (2 * LANE) * LANE),
                    1: (quarter // (2 * LANE) * LANE, quarter - quarter // (2 * LANE) * LANE),
                }[part]
                cols = pl.ds(pl.multiple_of(first + owner * quarter + low, LANE), count)
                if gather.y_first:
                    return buf.at[:, line, c, :, cols]
                return buf.at[line, :, c, :, cols]

            cols = pl.ds(first, RING * quarter)
            if gather.y_first:
                whole = buf.at[:, line, c, :, cols]
            else:
                whole = buf.at[line, :, c, :, cols]
            return Across(links, at, whole)

        return [ring(line) for line in gather.lines()]

    qx0, qdy0 = x0 + straight, dy0 + straight
    qa = piece(qx0 + t * quarter, quarter, True, False)
    qb = piece(qdy0 + t * quarter, quarter, False, False)
    xa, xb = across(qx0, qa), across(qdy0, qb)
    half = straight // (2 * LANE) * LANE
    p0 = piece(0, x0 + half, True)
    p1 = piece(x0 + half, straight - half, False)
    p2 = piece(dy0, half, True)
    p3 = piece(dy0 + half, straight - half, False)
    qa.one()
    qb.one()
    qa.two()
    qb.two()
    p0.one()
    p1.one()
    qa.three()
    xa[0].one()
    qb.three()
    xb[0].one()
    p0.two()
    p1.two()
    qa.four()
    xa[1].one()
    xa[2].one()
    qb.four()
    p0.three()
    p1.three()
    qa.five()
    xa[3].one()
    qb.five()
    p2.one()
    p3.one()
    xa[0].two()
    xb[1].one()
    xb[2].one()
    p2.two()
    p3.two()
    xa[1].two()
    xa[2].two()
    xb[3].one()
    p0.four()
    p1.four()
    p2.three()
    p3.three()
    xa[3].two()
    xa[0].three()
    xb[0].two()
    p0.five()
    p1.five()
    xa[1].three()
    xa[2].three()
    xb[1].two()
    xb[2].two()
    p0.six()
    p1.six()

    for copy in weights:
        copy.wait()
    my_slot = jnp.full((8, 1), me, jnp.int32)
    for g in range(RING):
        part = buf[g, :, :, :, pl.ds(0, LANE)].reshape(line, LANE)
        meta_all[pl.ds(g * line, line), :] = part
        row, gate, _ = entries(part, my_slot, per, cap, top)
        chosen = picks(row[0:1], group_rows)
        select[g] = chosen.astype(BF)
        gate_rows[pl.ds(g * group_rows, group_rows), :] = jnp.broadcast_to(
            jnp.sum(chosen * gate[0:1], axis=1, keepdims=True), (group_rows, LANE)
        )

    chunk = CHUNK

    def fill_rows(start):
        for g in range(RING):
            part = buf[g, :, :, :, pl.ds(start, chunk)].reshape(line, chunk)
            rows_buf[pl.ds(g * group_rows, group_rows), :] = dot(select[g], part).astype(BF)

    gate_acc[...] = jnp.zeros_like(gate_acc)
    up_acc[...] = jnp.zeros_like(up_acc)
    down_acc[...] = jnp.zeros_like(down_acc)

    def x_step(i, carry):
        off = pl.multiple_of(i * chunk, chunk)
        fill_rows(pl.multiple_of(x0 + i * chunk, LANE))
        gate_acc[...] += dot(rows_buf[...], wg[pl.ds(off, chunk), :])
        up_acc[...] += dot(rows_buf[...], wu[pl.ds(off, chunk), :])
        return carry

    def dy_step(i, carry):
        off = pl.multiple_of(i * chunk, chunk)
        fill_rows(pl.multiple_of(dy0 + i * chunk, LANE))
        down_acc[...] += dot(rows_buf[...], wd[pl.ds(off, chunk), :])
        return carry

    own = width // slots
    window = 3 * LANE
    low = jnp.minimum(lax.div(me * own, LANE) * LANE, width - window)
    shift = me * own - low
    move = jnp.where(
        lax.broadcasted_iota(jnp.int32, (window, 2 * LANE), 0)
        == lax.broadcasted_iota(jnp.int32, (window, 2 * LANE), 1) + shift,
        1.0,
        0.0,
    ).astype(BF)

    def cut(k, start):
        for g in range(RING):
            part = buf[g, :, :, :, pl.ds(pl.multiple_of(start + low, LANE), window)]
            cuts[k, pl.ds(g * line, line), :] = dot(part.reshape(line, window), move).astype(BF)

    strip = 32

    def silu_step(i, carry):
        r = pl.ds(pl.multiple_of(i * strip, strip), strip)
        gate_proj, up_proj = gate_acc[r, :], up_acc[r, :]
        sig = jax.nn.sigmoid(gate_proj)
        activated = gate_proj * sig
        acts[r, pl.ds(2 * ff, ff)] = (activated * up_proj).astype(BF)
        gate_acc[r, :] = up_proj * sig * (1.0 + gate_proj * (1.0 - sig))
        up_acc[r, :] = activated
        return carry

    def finish(i, carry):
        r = pl.ds(pl.multiple_of(i * strip, strip), strip)
        down_proj = down_acc[r, :]
        hidden_grad = gate_rows[r, 0:1] * down_proj
        acts[r, pl.ds(0, ff)] = (hidden_grad * gate_acc[r, :]).astype(BF)
        acts[r, pl.ds(ff, ff)] = (hidden_grad * up_acc[r, :]).astype(BF)
        hidden = acts[r, pl.ds(2 * ff, ff)].astype(F32)
        total = jnp.sum(hidden * down_proj, axis=1, keepdims=True)
        high = total.astype(BF)
        low_part = (total - high.astype(F32)).astype(BF)
        lanes = lax.broadcasted_iota(jnp.int32, (strip, LANE), 1)
        score[r, :] = jnp.where(
            lanes < LANE // 2, high.astype(F32), low_part.astype(F32)
        ).astype(BF)
        return carry

    steps, plain = width // chunk, straight // chunk
    strips = cap * slots // strip
    lax.fori_loop(0, plain, x_step, 0)
    p2.four()
    p3.four()
    xa[3].three()
    xb[0].three()
    xb[3].two()
    for ring in xa:
        ring.four()
    lax.fori_loop(plain, steps, x_step, 0)
    xb[1].three()
    xb[2].three()
    cut(0, x0)
    lax.fori_loop(0, strips, silu_step, 0)
    p2.five()
    p3.five()
    xb[3].three()
    for ring in xb:
        ring.four()
    lax.fori_loop(plain, steps, dy_step, 0)
    p2.six()
    p3.six()
    lax.fori_loop(0, plain, dy_step, 0)
    cut(1, dy0)
    lax.fori_loop(0, strips, finish, 0)
    links.drain()


def return_kernel(
    dims,
    acts, score, meta_all, cuts, w_gate, w_up,
    slot_grads, input_grads, gate_grads,
    held_all, wg, wu, far, up_buf, down_buf, far_in, sum_in, score_in,
    row_at, gate_at, rows_buf, turned, by_token, block_sum,
    y_far, y_sums, y_total, z_far, z_sums, z_total, stage,
    send, recv, local, out_sem,
):
    per, width, cap, top, ff = dims
    slots = RING * RING * CORES
    rows = cap * slots
    part = width // RING
    half = part // 2
    links = Links(send, recv)
    y, z, c, t = links.y, links.z, links.c, links.t
    a = acts
    me = lax.axis_index("expert")
    own = pltpu.make_async_copy(acts, held_all.at[y, z, c], local.at[0])
    weights = [
        pltpu.make_async_copy(w_gate, wg, local.at[2]),
        pltpu.make_async_copy(w_up, wu, local.at[3]),
    ]
    for copy in [own] + weights:
        copy.start()
    own.wait()
    right, left, across = links.to(t=up1(t)), links.to(t=down1(t)), links.to(t=up1(up1(t)))
    links.greet(links.plane() + [right, left, across])

    def piece(start, stop, y_first):
        middle = (start + stop) // 2
        spans = {None: (start, stop), 0: (start, middle), 1: (middle, stop)}

        def at(yy, zz, which):
            low, high = spans[which]
            return held_all.at[yy, zz, c, pl.ds(low, high - low), :]

        return Gather(links, at, y_first)

    group_rows = rows // RING
    line_tokens = per * slots // RING
    width_own = width // slots

    def place_rows():
        ids = lax.broadcasted_iota(jnp.int32, (slots, 1), 0)
        for g in range(RING):
            row, gate, _ = entries(
                meta_all[pl.ds(g * line_tokens, line_tokens), :], ids, per, cap, top
            )
            row_at[g] = row
            gate_at[g] = gate

    several = 4

    def turn_step(i, carry):
        for g in range(RING):
            toks = pl.ds(g * line_tokens, line_tokens)
            chosen, weighed = [], []
            for j in range(several):
                slot = i * several + j
                pick = picks(row_at[g, pl.ds(slot, 1), :], group_rows)
                chosen.append(pick.astype(BF))
                weighed.append((pick * gate_at[g, pl.ds(slot, 1), :]).astype(BF))
            for k, lhs in enumerate((chosen, weighed)):
                found = dot(jnp.concatenate(lhs, axis=0), cuts[k, toks, :])
                for j in range(several):
                    rows_buf[j, k, pl.ds(g * group_rows, group_rows), :] = found[
                        j * group_rows : (j + 1) * group_rows
                    ].astype(BF)
        for j in range(several):
            for k in range(2):
                turned[i * several + j, k] = jnp.transpose(rows_buf[j, k])[:width_own]
        return carry

    g0 = piece(0, rows // 2, True)
    g1 = piece(rows // 2, rows, False)
    g0.one()
    g1.one()
    for copy in weights:
        copy.wait()

    def fill(out, quarter, low, count, extra=None):
        r = pl.ds(pl.multiple_of(quarter * part + low, LANE), count)
        sums = dot(a[:, 0:ff], wg[r, :], NT) + dot(a[:, ff : 2 * ff], wu[r, :], NT)
        for more in extra or ():
            sums = sums + more[...].astype(F32)
        out[:, pl.ds(low, count)] = sums.astype(BF)

    pieces = []
    for low in (0, half):
        first = half // (2 * LANE) * LANE + LANE
        pieces.append(((low, first), (low + first, half - first)))

    def cols_of(span):
        return pl.ds(*span)

    far_copies, straight, summed = [], [], []

    def send_far(h):
        one, two = pieces[h]
        fill(far, up1(up1(t)), h * half, half)
        far_copies.append(
            (
                links.start(far.at[:, cols_of(one)], far_in.at[:, cols_of(one)], right),
                links.start(far.at[:, cols_of(two)], far_in.at[:, cols_of(two)], left),
            )
        )

    def send_straight(h):
        one, two = pieces[h]
        fill(up_buf, up1(t), *two)
        d_right = links.start(
            up_buf.at[:, cols_of(two)], sum_in.at[0, :, cols_of(two)], right
        )
        fill(down_buf, down1(t), *one)
        d_left = links.start(
            down_buf.at[:, cols_of(one)], sum_in.at[1, :, cols_of(one)], left
        )
        straight.append((d_right, d_left))

    def send_summed(h):
        one, two = pieces[h]
        f_right, f_left = far_copies[h]
        f_right.wait_recv()
        fill(up_buf, up1(t), *one, [far_in.at[:, cols_of(one)]])
        s_right = links.start(
            up_buf.at[:, cols_of(one)], sum_in.at[0, :, cols_of(one)], right
        )
        f_left.wait_recv()
        fill(down_buf, down1(t), *two, [far_in.at[:, cols_of(two)]])
        s_left = links.start(
            down_buf.at[:, cols_of(two)], sum_in.at[1, :, cols_of(two)], left
        )
        summed.append((s_right, s_left))

    wide = part + LANE
    shared, chosen_rows = [], []

    def to_tokens(h, score_rows=None):
        for copy in (*straight[h], *summed[h]):
            copy.wait_recv()
        cols = pl.ds(h * half, half)
        fill(far_in, t, h * half, half, [sum_in.at[0, :, cols], sum_in.at[1, :, cols]])
        low, stop = h * half, half if h == 0 else wide
        for g in range(RING):
            chosen = picks(row_at[g, pl.ds(me, 1), :], group_rows).astype(BF)
            r = pl.ds(g * group_rows, group_rows)
            found = dot(chosen, far_in[r, cols], TN).astype(BF)
            by_token[g, :, :, :, cols] = found.reshape(RING, CORES, per, half)
            if h == 1:
                named = meta_all[pl.ds(g * line_tokens, line_tokens), :].astype(F32)
                lanes = lax.broadcasted_iota(jnp.int32, (line_tokens, LANE), 1)
                found = dot(
                    chosen, score_rows[g * group_rows : (g + 1) * group_rows], TN
                )
                found = jnp.where((named == me.astype(F32)) & (lanes < top), found, 0.0)
                by_token[g, :, :, :, pl.ds(part, LANE)] = found.astype(BF).reshape(
                    RING, CORES, per, LANE
                )
        cols = pl.ds(low, stop - low)
        shared.append(
            links.start(
                by_token.at[:, :, 1 - c, :, cols], block_sum.at[:, :, :, cols], links.to(c=1 - c)
            )
        )

    def add_core(h):
        shared[h].wait_recv()
        low, stop = h * half, half if h == 0 else wide
        cols = pl.ds(low, stop - low)
        for g in range(RING):
            mine = by_token[g, :, pl.ds(c, 1), :, cols].reshape(RING, per, stop - low)
            block_sum[g, :, :, cols] = (
                block_sum[g, :, :, cols].astype(F32) + mine.astype(F32)
            ).astype(BF)

    rest = (wide - half) // 2
    spans = (
        (0, pieces[0][0][1], pieces[0][1][1]),
        (half, rest // 2, rest // 2),
        (half + rest, rest // 2, rest // 2),
    )
    firsts, seconds = [], []

    def ring_one(k):
        y_first = k < 2

        def at(v, lo, count):
            if y_first:
                return block_sum.at[v, :, :, pl.ds(lo, count)]
            return block_sum.at[:, v, :, pl.ds(lo, count)]

        firsts.append(
            RingSum(
                links,
                "y" if y_first else "z",
                at,
                lambda side, count: y_far.at[k, side, :, :, pl.ds(0, count)],
                lambda side, lo, count: y_sums.at[k, side, :, :, pl.ds(lo, count)],
                *spans[k],
            )
        )
        firsts[k].one()

    def ring_two(k):
        def put(lo, value):
            y_total[k, :, :, pl.ds(lo, value.shape[-1])] = value

        firsts[k].three(put)
        seconds.append(
            RingSum(
                links,
                "z" if k < 2 else "y",
                lambda v, lo, count: y_total.at[k, v, :, pl.ds(lo, count)],
                lambda side, count: z_far.at[k, side, :, pl.ds(0, count)],
                lambda side, lo, count: z_sums.at[k, side, :, pl.ds(lo, count)],
                0,
                *spans[k][1:],
            )
        )
        seconds[k].one()

    def ring_end(k):
        def put(lo, value):
            z_total[:, pl.ds(spans[k][0] + lo, value.shape[-1])] = value

        seconds[k].three(put)

    send_far(0)
    send_far(1)
    g0.two()
    g1.two()
    send_straight(0)
    place_rows()
    g0.three()
    g1.three()
    send_summed(0)
    send_straight(1)
    scores = [
        links.start(score, score_in.at[0], right),
        links.start(score, score_in.at[1], left),
        links.start(score, score_in.at[2], across),
    ]
    lax.fori_loop(0, slots // several // 2, turn_step, 0)
    send_summed(1)
    lax.fori_loop(slots // several // 2, slots // several, turn_step, 0)
    g0.four()
    g1.four()
    to_tokens(0)
    add_core(0)
    ring_one(0)
    for copy in scores:
        copy.wait_recv()
    total = jnp.zeros((rows, 1), F32)
    for ref in (score, score_in.at[0], score_in.at[1], score_in.at[2]):
        both = ref[...].astype(F32)
        total = total + (both[:, 0:1] + both[:, LANE // 2 : LANE // 2 + 1])
    score_rows = jnp.broadcast_to(total, (rows, LANE)).astype(BF)
    g0.five()
    g1.five()
    firsts[0].two()
    to_tokens(1, score_rows)
    ring_two(0)
    for gather in (g0, g1):
        gather.six()

    stored = []

    def grads(i):
        slot = i % 2
        if i >= 2:
            stored[i - 2].wait()

        def step(j, carry):
            place = (i // 2, (i % 2) * 2 + lax.div(j, CORES), lax.rem(j, CORES))
            own_slot = i * several + j
            both = dot(turned[own_slot, 0], held_all[(*place, slice(None), pl.ds(0, 2 * ff))])
            stage[slot, j, 0] = both[:, :ff].astype(BF)
            stage[slot, j, 1] = both[:, ff:].astype(BF)
            stage[slot, j, 2] = dot(
                turned[own_slot, 1], held_all[(*place, slice(None), pl.ds(2 * ff, ff))]
            ).astype(BF)
            return carry

        lax.fori_loop(0, several, step, 0)
        stored.append(
            pltpu.make_async_copy(
                stage.at[slot],
                slot_grads.at[pl.ds(i * several, several)],
                out_sem.at[i],
            )
        )
        stored[-1].start()

    grads(0)
    add_core(1)
    ring_one(1)
    ring_one(2)
    seconds[0].two()
    grads(1)
    grads(2)
    firsts[1].two()
    firsts[2].two()
    grads(3)
    grads(4)
    ring_two(1)
    ring_two(2)
    grads(5)
    seconds[1].two()
    seconds[2].two()
    grads(6)
    for k in range(3):
        ring_end(k)
    input_grads[...] = z_total[:, pl.ds(0, part)]
    gate_grads[...] = z_total[:, pl.ds(part, LANE)]
    grads(7)
    links.drain()
    stored[-2].wait()
    stored[-1].wait()


def combine_kernel(replicas, owners, slot_grads, out, copies, held, sems):
    experts = out.shape[0]
    load = pltpu.make_async_copy(
        slot_grads.at[pl.ds(experts, replicas)], copies, sems.at[2 * experts]
    )
    load.start()
    loads, stores = [], []
    for e in range(experts):
        loads.append(pltpu.make_async_copy(slot_grads.at[e], held.at[e], sems.at[e]))
        stores.append(pltpu.make_async_copy(held.at[e], out.at[e], sems.at[experts + e]))
        loads[e].start()
    load.wait()
    for e in range(experts):
        loads[e].wait()
        owned = owners[0] == e
        for r in range(1, replicas):
            owned = owned | (owners[r] == e)

        @pl.when(owned)
        def _():
            for k in range(3):
                total = held[e, k].astype(F32)
                for r in range(replicas):
                    same = jnp.where(owners[r] == e, 1.0, 0.0)
                    total = total + same * copies[r, k].astype(F32)
                held[e, k] = total.astype(BF)

        stores[e].start()
    for store in stores:
        store.wait()


def per_device(tokens, cotangent, gate_weights, route_slots, replica_owner, w_gate, w_up, w_down):
    slots = lax.axis_size("expert")
    per, width = tokens.shape
    top = route_slots.shape[1]
    cap = per * top * 3 // 2 // slots
    ff = w_gate.shape[2]
    rows = cap * slots
    part = width // RING
    padded = 16
    replicas = replica_owner.shape[0]
    experts = slots - replicas
    dims = (per, width, cap, top, ff)
    meta = jnp.concatenate(
        [
            route_slots.astype(BF),
            gate_weights,
            jnp.full((per, LANE - 2 * top), -1, BF),
        ],
        axis=1,
    )
    w_gate, w_up, w_down = w_gate[0], w_up[0], w_down[0]
    any_ = pl.BlockSpec(memory_space=pl.ANY)
    vmem = pl.BlockSpec(memory_space=pltpu.VMEM)
    line = per * slots // RING
    copies = 4 * GATHER_COPIES + 2 * (GATHER_COPIES - 4) + 8 * ACROSS_COPIES
    acts, score, cuts, meta_all = pl.pallas_call(
        functools.partial(dispatch_kernel, dims),
        name="dispatch",
        out_shape=(
            jax.ShapeDtypeStruct((rows, 3 * ff), BF),
            jax.ShapeDtypeStruct((rows, LANE), BF),
            jax.ShapeDtypeStruct((2, per * slots, 2 * LANE), BF),
            jax.ShapeDtypeStruct((per * slots, LANE), BF),
        ),
        in_specs=[any_] * 6,
        out_specs=(vmem,) * 4,
        scratch_shapes=[
            pltpu.VMEM((RING, RING, CORES, per, LANE + 2 * width), BF),
            pltpu.VMEM((width, ff), BF),
            pltpu.VMEM((width, ff), BF),
            pltpu.VMEM((width, ff), BF),
            pltpu.VMEM((rows, CHUNK), BF),
            pltpu.VMEM((rows, ff), F32),
            pltpu.VMEM((rows, ff), F32),
            pltpu.VMEM((rows, ff), F32),
            pltpu.VMEM((RING, rows // RING, line), BF),
            pltpu.VMEM((rows, LANE), F32),
            pltpu.SemaphoreType.DMA((copies,)),
            pltpu.SemaphoreType.DMA((copies,)),
            pltpu.SemaphoreType.DMA((6,)),
        ],
        compiler_params=pltpu.CompilerParams(
            collective_id=0, has_side_effects=True, vmem_limit_bytes=56 * MIB
        ),
    )(tokens, cotangent, meta, w_gate, w_up, w_down)
    copies = 2 * GATHER_COPIES + 15 + 2 + 6 * RING_COPIES
    own = width // slots
    wide = part + LANE
    half = part // 2
    piece = half // (2 * LANE) * LANE + LANE
    slot_grads, input_grads, gate_grads = pl.pallas_call(
        functools.partial(return_kernel, dims),
        name="grads_back",
        out_shape=(
            jax.ShapeDtypeStruct((slots, 3, own, ff), BF),
            jax.ShapeDtypeStruct((per, part), BF),
            jax.ShapeDtypeStruct((per, LANE), BF),
        ),
        in_specs=[vmem, vmem, vmem, vmem, any_, any_],
        out_specs=(any_, vmem, vmem),
        scratch_shapes=[
            pltpu.VMEM((RING, RING, CORES, rows, 3 * ff), BF),
            pltpu.VMEM((width, ff), BF),
            pltpu.VMEM((width, ff), BF),
            pltpu.VMEM((rows, part), BF),
            pltpu.VMEM((rows, part), BF),
            pltpu.VMEM((rows, part), BF),
            pltpu.VMEM((rows, part), BF),
            pltpu.VMEM((2, rows, part), BF),
            pltpu.VMEM((3, rows, LANE), BF),
            pltpu.VMEM((RING, slots, line), F32),
            pltpu.VMEM((RING, slots, line), F32),
            pltpu.VMEM((4, 2, rows, 2 * LANE), BF),
            pltpu.VMEM((slots, 2, own, rows), BF),
            pltpu.VMEM((RING, RING, CORES, per, wide), BF),
            pltpu.VMEM((RING, RING, per, wide), BF),
            pltpu.VMEM((3, 2, RING, per, piece), BF),
            pltpu.VMEM((3, 2, RING, per, half), BF),
            pltpu.VMEM((3, RING, per, half), BF),
            pltpu.VMEM((3, 2, per, piece), BF),
            pltpu.VMEM((3, 2, per, half), BF),
            pltpu.VMEM((per, wide), BF),
            pltpu.VMEM((2, 4, 3, own, ff), BF),
            pltpu.SemaphoreType.DMA((copies,)),
            pltpu.SemaphoreType.DMA((copies,)),
            pltpu.SemaphoreType.DMA((4,)),
            pltpu.SemaphoreType.DMA((slots // 4,)),
        ],
        compiler_params=pltpu.CompilerParams(
            collective_id=1, has_side_effects=True, vmem_limit_bytes=62 * MIB
        ),
    )(acts, score, meta_all, cuts, w_gate, w_up)
    expert_grads = pl.pallas_call(
        functools.partial(combine_kernel, replicas),
        name="combine",
        out_shape=jax.ShapeDtypeStruct((experts, 3, own, ff), BF),
        in_specs=[pl.BlockSpec(memory_space=pltpu.SMEM), any_],
        out_specs=any_,
        scratch_shapes=[
            pltpu.VMEM((replicas, 3, own, ff), BF),
            pltpu.VMEM((experts, 3, own, ff), BF),
            pltpu.SemaphoreType.DMA((2 * experts + 1,)),
        ],
        compiler_params=pltpu.CompilerParams(vmem_limit_bytes=60 * MIB),
    )(replica_owner, slot_grads)
    return input_grads, gate_grads[:, :top], jnp.transpose(expert_grads, (0, 2, 1, 3))


def solution(mesh):
    in_specs = (
        P("expert", None),
        P("expert", None),
        P("expert", None),
        P("expert", None),
        P(),
        P("expert", None, "tensor"),
        P("expert", None, "tensor"),
        P("expert", None, "tensor"),
    )
    out_specs = (P("expert", "tensor"), P("expert", None), P(None, "expert", None, "tensor"))
    return jax.shard_map(
        per_device, mesh=mesh, in_specs=in_specs, out_specs=out_specs, check_vma=False
    )
```
